32 devices in a mesh: slab: 4 (over y, x), row: 8 (over z, core).
Axes of the slice: x: 2, y: 2, z: 4, core: 2. Of those that a mesh axis runs over, the one named last changes fastest.
Arguments:
- forcing: bfloat16 [4, 4096, 64], P('slab', 'row'), may hold values from -6 to 6
- inflow: bfloat16 [4096, 64], P('row'), may hold values from -6 to 6
- self_solve: bfloat16 [4, 8, 512, 512], P('slab', 'row'), may hold values from -0.25 to 0.25
- greens: bfloat16 [4, 8, 8, 512, 512], P('slab', 'row'), may hold values from -0.125 to 0.125
- kept_cols: int32 [4, 8, 8], P('slab', 'row'), may hold values from 0 to 7, as said below
- counts: int32 [4, 8], P('slab', 'row'), may hold values from 2 to 8, as said below
Outputs:
- traces: bfloat16 [4, 4096, 64], P('slab', 'row')
The draws below stay inside these ranges and needn't reach their ends.
Inputs may be any that keep to these rules, and one draw needn't show every extreme that they name: `kept_cols`: for each slab and tile row the 8 entries name distinct column tiles. `counts`: in every slab some tile row uses all 8 slots.
All inputs are finite; a program needn't handle non-finite values.
Results may differ from the reference program's by a relative error of at most 0.012.
Values may be sent and summed in bfloat16 or wider, within the bound.
No kernel may reach another device: no remote copies, remote signals or barrier semaphores. Data moves between devices by JAX's collectives and lax.ppermute only.
A program may use at most 64 MiB of HBM per device.

```python
import jax
import jax.numpy as jnp
from jax import lax

TILE = 512
N_SLABS = 4
NT = 8
KMAX = 8
NTR = 4096
RHS = 64


def draw_kept_cols(key, part):
    sub = jax.random.fold_in(key, 11)
    scores = jax.random.randint(sub, (N_SLABS, NT, NT), 0, 1 << 20) * NT + jnp.arange(NT, dtype=jnp.int32)
    order = jnp.argsort(scores, axis=-1, stable=True).astype(jnp.int32)
    return order[:, :, :KMAX]


def draw_counts(key, part):
    sub = jax.random.fold_in(key, 23)
    lower = max(1, KMAX // 3)
    values = jax.random.randint(sub, (N_SLABS, NT), lower, KMAX + 1)
    chosen = jax.random.randint(jax.random.fold_in(key, 37), (N_SLABS,), 0, NT)
    places = jnp.arange(NT, dtype=jnp.int32)[None, :]
    return jnp.where(places == chosen[:, None], KMAX, values).astype(jnp.int32)


def shard_levels(own_key, shape, shards, low, high):
    def one(position, shards_of):
        draws = jax.random.uniform(jax.random.fold_in(jax.random.fold_in(own_key, 6), position), (shards_of,), jnp.float32, low / len(shards), high / len(shards))
        return jnp.repeat(jnp.exp(draws), shape[position] // shards_of).reshape((-1,) + (1,) * (len(shape) - position - 1))

    loudness = one(*shards[0])
    for cut in shards[1:]:
        loudness = loudness * one(*cut)
    return loudness


def gaussian(rng, extent, deviation, limit, split=(), held_as=jnp.bfloat16):
    result = jax.random.normal(rng, extent, jnp.float32) * deviation
    if len(split) > 0:
        result = shard_levels(rng, extent, split, -0.22, 0.18) * result
    return jnp.clip(result, min=-limit, max=limit).astype(held_as)


def setup_inputs(seed: int = 0) -> dict:
    key_list = jax.random.split(jax.random.key(seed), 7)
    forcing = gaussian(key_list[0], (N_SLABS, NTR, RHS), 1.0, 6.0, ((0, 4), (1, 8)))
    inflow = gaussian(key_list[1], (NTR, RHS), 1.0, 6.0, ((0, 8),))
    self_solve = gaussian(key_list[2], (N_SLABS, NT, TILE, TILE), TILE ** -0.5, 0.25, ((0, 4), (1, 8)))
    greens = gaussian(key_list[3], (N_SLABS, NT, KMAX, TILE, TILE), (KMAX * TILE // 2 + TILE) ** -0.5, 0.125, ((0, 4), (1, 8)))
    kept_cols = draw_kept_cols(jax.random.fold_in(key_list[6], 71), 0)
    counts = draw_counts(jax.random.fold_in(key_list[6], 71), 0)
    return {"forcing": forcing, "inflow": inflow, "self_solve": self_solve, "greens": greens, "kept_cols": kept_cols, "counts": counts}


def reference(forcing, inflow, self_solve, greens, kept_cols, counts):
    incoming = inflow
    columns = inflow.shape[1]
    results = []
    slot_ids = jnp.arange(KMAX, dtype=jnp.int32)
    for slab_index in range(N_SLABS):
        tiles = incoming.reshape(NT, TILE, columns)
        sources = forcing[slab_index].reshape(NT, TILE, columns)

        def one_row(items):
            green_row, cols_row, count_row, solve_row, source_row = items
            chosen = tiles[cols_row]
            valid = slot_ids < count_row
            chosen = jnp.where(valid[:, None, None], chosen, jnp.zeros((), chosen.dtype))
            total = jnp.einsum("kij,kjw->iw", green_row.astype(jnp.float32), chosen.astype(jnp.float32))
            coupled = (total + source_row.astype(jnp.float32)).astype(jnp.bfloat16)
            return jnp.dot(solve_row, coupled, preferred_element_type=jnp.float32).astype(jnp.bfloat16)

        outgoing = lax.map(one_row, (greens[slab_index], kept_cols[slab_index], counts[slab_index], self_solve[slab_index], sources))
        outgoing = outgoing.reshape(NT * TILE, columns)
        results.append(outgoing)
        incoming = outgoing
    return jnp.stack(results, axis=0)
```

```python
import functools

import jax
import jax.numpy as jnp
from jax import lax
from jax.experimental import pallas as pl
from jax.experimental.pallas import tpu as pltpu
from jax.sharding import PartitionSpec as P

CORES = 2
VMEM_LIMIT = 48 * 2**20
CONTRACT_LAST = (((1,), (1,)), ((), ()))
IN_VMEM = pl.BlockSpec(memory_space=pltpu.VMEM)
IN_SMEM = pl.BlockSpec(memory_space=pltpu.SMEM)
ANYWHERE = pl.BlockSpec(memory_space=pl.ANY)


def params():
    return pltpu.CompilerParams(vmem_limit_bytes=VMEM_LIMIT)


def place_kernel(chips, cols_ref, count_ref, greens_ref, placed_ref, sems):
    slots, positions = greens_ref.shape[0], placed_ref.shape[0]
    me = lax.axis_index("row")
    chip, core = me // CORES, me % CORES
    if positions > slots:
        placed_ref[...] = jnp.zeros_like(placed_ref)
    copies = []
    for slot in range(slots):
        column = cols_ref[slot]
        hop = lax.rem(chip - column // CORES + chips, chips)
        position = jnp.where(column % CORES == core, 0, chips) + hop
        copy = pltpu.make_async_copy(greens_ref.at[slot], placed_ref.at[position], sems.at[slot])
        used = slot < count_ref[0]
        copies.append((used, copy))

        @pl.when(used)
        def _():
            copy.start()

        if positions == slots:

            @pl.when(jnp.logical_not(used))
            def _():
                placed_ref[position] = jnp.zeros(placed_ref.shape[1:], placed_ref.dtype)

    for used, copy in copies:

        @pl.when(used)
        def _():
            copy.wait()


def place(chips, cols, count, greens):
    slots, rows, depth = greens.shape
    return pl.pallas_call(
        functools.partial(place_kernel, chips),
        out_shape=pltpu.VMEM((chips * CORES, rows, depth), greens.dtype),
        in_specs=[IN_SMEM, IN_SMEM, ANYWHERE],
        out_specs=IN_VMEM,
        scratch_shapes=[pltpu.SemaphoreType.DMA((slots,))],
        compiler_params=params(),
        name="place",
    )(cols, count, greens)


def products(tiles, placed_ref, first):
    total = None
    for offset, tile in enumerate(tiles):
        term = lax.dot_general(
            tile[...], placed_ref[first + offset], CONTRACT_LAST, preferred_element_type=jnp.float32
        )
        total = term if total is None else total + term
    return total


def early_kernel(section, placed_ref, *refs):
    tiles, total_ref = refs[:-1], refs[-1]

    @pl.when(lax.axis_index("slab") == section)
    def _():
        total_ref[...] = products(tiles, placed_ref, 0)


def early(section, placed, tiles):
    return pl.pallas_call(
        functools.partial(early_kernel, section),
        out_shape=pltpu.VMEM(tiles[0].shape, jnp.float32),
        in_specs=[IN_VMEM] * (1 + len(tiles)),
        out_specs=IN_VMEM,
        compiler_params=params(),
        name="early_tiles",
    )(placed, *tiles)


def late_kernel(section, placed_ref, total_ref, tile_ref, source_ref, solve_ref, trace_in, trace_ref):
    @pl.when(lax.axis_index("slab") == section)
    def _():
        total = total_ref[...] + products([tile_ref], placed_ref, placed_ref.shape[0] - 1)
        coupled = (total + source_ref[...].astype(jnp.float32)).astype(jnp.bfloat16)
        trace_ref[...] = lax.dot_general(
            coupled, solve_ref[...], CONTRACT_LAST, preferred_element_type=jnp.float32
        ).astype(trace_ref.dtype)


def late(section, placed, total, tile, source, solve, trace):
    return pl.pallas_call(
        functools.partial(late_kernel, section),
        out_shape=pltpu.VMEM(trace.shape, trace.dtype),
        in_specs=[IN_VMEM] * 6,
        out_specs=IN_VMEM,
        input_output_aliases={5: 0},
        compiler_params=params(),
        name="late_tile_and_solve",
    )(placed, total, tile, source, solve, trace)


def swapped(tile, rows):
    return lax.ppermute(tile, "row", [(r, r ^ 1) for r in range(rows)])


def direct(forcing, inflow, self_solve, greens, kept_cols, counts):
    slabs, rows = lax.axis_size("slab"), lax.axis_size("row")
    chips = rows // CORES
    placed = place(chips, kept_cols[0, 0], counts[0], greens[0, 0])
    source = forcing[0].T
    solve = self_solve[0, 0]
    trace = inflow.T
    own = [trace]
    for hop in range(1, chips):
        own.append(lax.ppermute(trace, "row", [(r, (r + hop * CORES) % rows) for r in range(rows)]))
    for section in range(slabs):
        if section > 0:
            before, now = (section - 1) * rows, section * rows
            own = [
                lax.ppermute(
                    trace, ("slab", "row"), [(before + r, now + (r + hop * CORES) % rows) for r in range(rows)]
                )
                for hop in range(chips)
            ]
        other = [swapped(tile, rows) for tile in own]
        total = early(section, placed, own + other[:-1])
        trace = late(section, placed, total, other[-1], source, solve, trace)
    return trace.T[None]


def shifted(array, axis, by):
    size = lax.axis_size(axis)
    return lax.ppermute(array, axis, [(i, i + by) for i in range(size) if 0 <= i + by < size])


def gathering(forcing, inflow, self_solve, greens, kept_cols, counts):
    source, green_row, solve = forcing[0], greens[0, 0], self_solve[0, 0]
    valid = jnp.arange(green_row.shape[0], dtype=jnp.int32) < counts[0, 0]
    incoming = inflow
    for section in range(lax.axis_size("slab")):
        if section > 0:
            arrived = shifted(trace, "slab", 1)
            incoming = jnp.where(lax.axis_index("slab") == 0, inflow, arrived)
        gathered = lax.all_gather(incoming, "row", axis=0)
        chosen = gathered[kept_cols[0, 0]]
        chosen = jnp.where(valid[:, None, None], chosen, jnp.zeros((), chosen.dtype))
        total = jnp.einsum("kij,kjw->iw", green_row, chosen, preferred_element_type=jnp.float32)
        coupled = (total + source.astype(jnp.float32)).astype(jnp.bfloat16)
        trace = jnp.dot(solve, coupled, preferred_element_type=jnp.float32).astype(jnp.bfloat16)
    return trace[None]


def shards(forcing, inflow, self_solve, greens, kept_cols, counts):
    rows, slots = lax.axis_size("row"), greens.shape[2]
    if rows % CORES == 0 and rows <= 2 * slots:
        return direct(forcing, inflow, self_solve, greens, kept_cols, counts)
    return gathering(forcing, inflow, self_solve, greens, kept_cols, counts)


def solution(mesh):
    placed = (
        P("slab", "row", None),
        P("row", None),
        P("slab", "row", None, None),
        P("slab", "row", None, None, None),
        P("slab", "row", None),
        P("slab", "row"),
    )
    return jax.shard_map(
        shards, mesh=mesh, in_specs=placed, out_specs=P("slab", "row", None), check_vma=False
    )
```

```python
import functools

import jax
import jax.numpy as jnp
from jax import lax
from jax.experimental import pallas as pl
from jax.experimental.pallas import tpu as pltpu
from jax.sharding import PartitionSpec as P

CORES = 2
VMEM_LIMIT = 48 * 2**20
CONTRACT_LAST = (((1,), (1,)), ((), ()))
IN_VMEM = pl.BlockSpec(memory_space=pltpu.VMEM)
IN_SMEM = pl.BlockSpec(memory_space=pltpu.SMEM)
ANYWHERE = pl.BlockSpec(memory_space=pl.ANY)


def params():
    return pltpu.CompilerParams(vmem_limit_bytes=VMEM_LIMIT)


def step_of(order, chips):
    return chips - 1 - order


def order_of(step, chips):
    return chips - 1 - step


def place_kernel(chips, cols_ref, count_ref, greens_ref, placed_ref, sems):
    slots, positions = greens_ref.shape[0], placed_ref.shape[0]
    me = lax.axis_index("row")
    chip, core = me // CORES, me % CORES
    if positions > slots:
        placed_ref[...] = jnp.zeros_like(placed_ref)
    copies = []
    for slot in range(slots):
        column = cols_ref[slot]
        order = order_of(chip ^ (column // CORES), chips)
        position = jnp.where(column % CORES == core, 0, chips) + order
        copy = pltpu.make_async_copy(greens_ref.at[slot], placed_ref.at[position], sems.at[slot])
        used = slot < count_ref[0]
        copies.append((used, copy))

        @pl.when(used)
        def _():
            copy.start()

        if positions == slots:

            @pl.when(jnp.logical_not(used))
            def _():
                placed_ref[position] = jnp.zeros(placed_ref.shape[1:], placed_ref.dtype)

    for used, copy in copies:

        @pl.when(used)
        def _():
            copy.wait()


def place(chips, cols, count, greens):
    slots, rows, depth = greens.shape
    return pl.pallas_call(
        functools.partial(place_kernel, chips),
        out_shape=pltpu.VMEM((chips * CORES, rows, depth), greens.dtype),
        in_specs=[IN_SMEM, IN_SMEM, ANYWHERE],
        out_specs=IN_VMEM,
        scratch_shapes=[pltpu.SemaphoreType.DMA((slots,))],
        compiler_params=params(),
        cost_estimate=pl.CostEstimate(flops=0, bytes_accessed=2 * greens.size * 2, transcendentals=0),
        name="place",
    )(cols, count, greens)


def products(tiles, placed_ref, first):
    total = None
    for offset, tile in enumerate(tiles):
        term = lax.dot_general(
            tile[...], placed_ref[first + offset], CONTRACT_LAST, preferred_element_type=jnp.float32
        )
        total = term if total is None else total + term
    return total


def early_kernel(section, placed_ref, *refs):
    tiles, total_ref = refs[:-1], refs[-1]

    @pl.when(lax.axis_index("slab") == section)
    def _():
        total_ref[...] = products(tiles, placed_ref, 0)


def early(section, placed, tiles):
    return pl.pallas_call(
        functools.partial(early_kernel, section),
        out_shape=pltpu.VMEM(tiles[0].shape, jnp.float32),
        in_specs=[IN_VMEM] * (1 + len(tiles)),
        out_specs=IN_VMEM,
        compiler_params=params(),
        name="early_tiles",
    )(placed, *tiles)


def late_kernel(section, placed_ref, total_ref, tile_ref, source_ref, solve_ref, trace_in, trace_ref):
    @pl.when(lax.axis_index("slab") == section)
    def _():
        total = total_ref[...] + products([tile_ref], placed_ref, placed_ref.shape[0] - 1)
        coupled = (total + source_ref[...].astype(jnp.float32)).astype(jnp.bfloat16)
        trace_ref[...] = lax.dot_general(
            coupled, solve_ref[...], CONTRACT_LAST, preferred_element_type=jnp.float32
        ).astype(trace_ref.dtype)


def late(section, placed, total, tile, source, solve, trace):
    return pl.pallas_call(
        functools.partial(late_kernel, section),
        out_shape=pltpu.VMEM(trace.shape, trace.dtype),
        in_specs=[IN_VMEM] * 6,
        out_specs=IN_VMEM,
        input_output_aliases={5: 0},
        compiler_params=params(),
        name="late_tile_and_solve",
    )(placed, total, tile, source, solve, trace)


def swapped(tile, rows):
    return lax.ppermute(tile, "row", [(r, r ^ 1) for r in range(rows)])


def sent(tile, source, target, step, slabs, rows, via=None):
    pairs = [(source * rows + r, target * rows + (r ^ (step * CORES))) for r in range(rows)]
    busy = {source, target}
    if source != target and via is not None:
        pairs += [(target * rows + r, via * rows + r) for r in range(rows)]
        pairs += [(via * rows + r, source * rows + r) for r in range(rows)]
        busy.add(via)
    if source == target or via is not None:
        pairs += [(s * rows + r, s * rows + (r ^ 1)) for s in range(slabs) if s not in busy for r in range(rows)]
    return lax.ppermute(tile, ("slab", "row"), pairs)


def direct(forcing, inflow, self_solve, greens, kept_cols, counts):
    slabs, rows = lax.axis_size("slab"), lax.axis_size("row")
    chips = rows // CORES
    steps = [step_of(order, chips) for order in range(chips)]
    placed = place(chips, kept_cols[0, 0], counts[0], greens[0, 0])
    source = forcing[0].T
    solve = self_solve[0, 0]
    trace = jnp.zeros(source.shape, jnp.bfloat16)
    entering = inflow.T
    for section in range(slabs):
        if section == 0:
            own = [sent(entering, 0, 0, step, slabs, rows) if step else entering for step in steps]
            placed, source, solve, *own = lax.optimization_barrier((placed, source, solve, *own))
        else:
            others = [s % slabs for s in range(section + 1, section + slabs - 1)]
            others += [None] * (chips - len(others))
            own = [
                sent(trace, section - 1, section, step, slabs, rows, via)
                for step, via in zip(steps, others)
            ]
        other = [swapped(tile, rows) for tile in own]
        total = early(section, placed, own + other[:-1])
        trace = late(section, placed, total, other[-1], source, solve, trace)
    return trace.T[None]


def shifted(array, axis, by):
    size = lax.axis_size(axis)
    return lax.ppermute(array, axis, [(i, i + by) for i in range(size) if 0 <= i + by < size])


def gathering(forcing, inflow, self_solve, greens, kept_cols, counts):
    source, green_row, solve = forcing[0], greens[0, 0], self_solve[0, 0]
    valid = jnp.arange(green_row.shape[0], dtype=jnp.int32) < counts[0, 0]
    incoming = inflow
    for section in range(lax.axis_size("slab")):
        if section > 0:
            arrived = shifted(trace, "slab", 1)
            incoming = jnp.where(lax.axis_index("slab") == 0, inflow, arrived)
        gathered = lax.all_gather(incoming, "row", axis=0)
        chosen = gathered[kept_cols[0, 0]]
        chosen = jnp.where(valid[:, None, None], chosen, jnp.zeros((), chosen.dtype))
        total = jnp.einsum("kij,kjw->iw", green_row, chosen, preferred_element_type=jnp.float32)
        coupled = (total + source.astype(jnp.float32)).astype(jnp.bfloat16)
        trace = jnp.dot(solve, coupled, preferred_element_type=jnp.float32).astype(jnp.bfloat16)
    return trace[None]


def shards(forcing, inflow, self_solve, greens, kept_cols, counts):
    rows, slots = lax.axis_size("row"), greens.shape[2]
    chips = rows // CORES
    if rows == chips * CORES and chips & (chips - 1) == 0 and rows <= 2 * slots:
        return direct(forcing, inflow, self_solve, greens, kept_cols, counts)
    return gathering(forcing, inflow, self_solve, greens, kept_cols, counts)


def solution(mesh):
    placed = (
        P("slab", "row", None),
        P("row", None),
        P("slab", "row", None, None),
        P("slab", "row", None, None, None),
        P("slab", "row", None),
        P("slab", "row"),
    )
    return jax.shard_map(
        shards, mesh=mesh, in_specs=placed, out_specs=P("slab", "row", None), check_vma=False
    )
```

```python
import functools

import jax
import jax.numpy as jnp
from jax import lax
from jax.experimental import pallas as pl
from jax.experimental.pallas import tpu as pltpu
from jax.sharding import PartitionSpec as P

CORES = 2
VMEM_LIMIT = 48 * 2**20
CONTRACT_LAST = (((1,), (1,)), ((), ()))
IN_VMEM = pl.BlockSpec(memory_space=pltpu.VMEM)
IN_SMEM = pl.BlockSpec(memory_space=pltpu.SMEM)
ANYWHERE = pl.BlockSpec(memory_space=pl.ANY)


def params():
    return pltpu.CompilerParams(vmem_limit_bytes=VMEM_LIMIT)


def step_of(order, chips):
    half = chips // 2
    return half + order // 2 if order % 2 == 0 else half - 1 - order // 2


def order_of(step, chips):
    half = chips // 2
    return jnp.where(step >= half, 2 * (step - half), 2 * (half - 1 - step) + 1)


def place_kernel(chips, cols_ref, count_ref, greens_ref, placed_ref, sems):
    slots, positions = greens_ref.shape[0], placed_ref.shape[0]
    me = lax.axis_index("row")
    chip, core = me // CORES, me % CORES
    if positions > slots:
        placed_ref[...] = jnp.zeros_like(placed_ref)
    copies = []
    for slot in range(slots):
        column = cols_ref[slot]
        order = order_of(chip ^ (column // CORES), chips)
        position = jnp.where(column % CORES == core, 0, chips) + order
        copy = pltpu.make_async_copy(greens_ref.at[slot], placed_ref.at[position], sems.at[slot])
        used = slot < count_ref[0]
        copies.append((used, copy))

        @pl.when(used)
        def _():
            copy.start()

        if positions == slots:

            @pl.when(jnp.logical_not(used))
            def _():
                placed_ref[position] = jnp.zeros(placed_ref.shape[1:], placed_ref.dtype)

    for used, copy in copies:

        @pl.when(used)
        def _():
            copy.wait()


def place(chips, cols, count, greens):
    slots, rows, depth = greens.shape
    return pl.pallas_call(
        functools.partial(place_kernel, chips),
        out_shape=pltpu.VMEM((chips * CORES, rows, depth), greens.dtype),
        in_specs=[IN_SMEM, IN_SMEM, ANYWHERE],
        out_specs=IN_VMEM,
        scratch_shapes=[pltpu.SemaphoreType.DMA((slots,))],
        compiler_params=params(),
        cost_estimate=pl.CostEstimate(flops=0, bytes_accessed=2 * greens.size * 2, transcendentals=0),
        name="place",
    )(cols, count, greens)


def products(tiles, placed_ref, first):
    total = None
    for offset, tile in enumerate(tiles):
        term = lax.dot_general(
            tile[...], placed_ref[first + offset], CONTRACT_LAST, preferred_element_type=jnp.float32
        )
        total = term if total is None else total + term
    return total


def early_kernel(section, placed_ref, *refs):
    tiles, total_ref = refs[:-1], refs[-1]

    @pl.when(lax.axis_index("slab") == section)
    def _():
        total_ref[...] = products(tiles, placed_ref, 0)


def early(section, placed, tiles):
    return pl.pallas_call(
        functools.partial(early_kernel, section),
        out_shape=pltpu.VMEM(tiles[0].shape, jnp.float32),
        in_specs=[IN_VMEM] * (1 + len(tiles)),
        out_specs=IN_VMEM,
        compiler_params=params(),
        name="early_tiles",
    )(placed, *tiles)


def late_kernel(section, placed_ref, total_ref, tile_ref, source_ref, solve_ref, trace_in, trace_ref):
    @pl.when(lax.axis_index("slab") == section)
    def _():
        total = total_ref[...] + products([tile_ref], placed_ref, placed_ref.shape[0] - 1)
        coupled = (total + source_ref[...].astype(jnp.float32)).astype(jnp.bfloat16)
        trace_ref[...] = lax.dot_general(
            coupled, solve_ref[...], CONTRACT_LAST, preferred_element_type=jnp.float32
        ).astype(trace_ref.dtype)


def late(section, placed, total, tile, source, solve, trace):
    return pl.pallas_call(
        functools.partial(late_kernel, section),
        out_shape=pltpu.VMEM(trace.shape, trace.dtype),
        in_specs=[IN_VMEM] * 6,
        out_specs=IN_VMEM,
        input_output_aliases={5: 0},
        compiler_params=params(),
        name="late_tile_and_solve",
    )(placed, total, tile, source, solve, trace)


def swapped(tile, rows):
    return lax.ppermute(tile, "row", [(r, r ^ 1) for r in range(rows)])


def sent(tile, source, target, step, slabs, rows, via=None):
    pairs = [(source * rows + r, target * rows + (r ^ (step * CORES))) for r in range(rows)]
    busy = {source, target}
    if source != target and via is not None:
        pairs += [(target * rows + r, via * rows + (r if via != source else r ^ (step * CORES))) for r in range(rows)]
    if via not in (None, source):
        pairs += [(via * rows + r, source * rows + r) for r in range(rows)]
    if via is not None:
        busy.add(via)
        pairs += [(s * rows + r, s * rows + (r ^ 1)) for s in range(slabs) if s not in busy for r in range(rows)]
    return lax.ppermute(tile, ("slab", "row"), pairs)


def third_slabs(section, slabs, chips):
    free = [s % slabs for s in range(section + 1, section + slabs - 1)]
    free = [s for s in free if s != section - 2][: chips - 1]
    return free + [None] * (chips - 1 - len(free)) + [section - 1]


def direct(forcing, inflow, self_solve, greens, kept_cols, counts):
    slabs, rows = lax.axis_size("slab"), lax.axis_size("row")
    chips = rows // CORES
    steps = [step_of(order, chips) for order in range(chips)]
    placed = place(chips, kept_cols[0, 0], counts[0], greens[0, 0])
    source = forcing[0].T
    solve = self_solve[0, 0]
    trace = jnp.zeros(source.shape, jnp.bfloat16)
    entering = inflow.T
    for section in range(slabs):
        if section == 0:
            own = [sent(entering, 0, 0, step, slabs, rows, 0) if step else entering for step in steps]
            placed, source, solve, *own = lax.optimization_barrier((placed, source, solve, *own))
        else:
            vias = third_slabs(section, slabs, chips)
            own = [sent(trace, section - 1, section, step, slabs, rows, via) for step, via in zip(steps, vias)]
        other = [swapped(tile, rows) for tile in own]
        total = early(section, placed, own + other[:-1])
        trace = late(section, placed, total, other[-1], source, solve, trace)
    return trace.T[None]


def shifted(array, axis, by):
    size = lax.axis_size(axis)
    return lax.ppermute(array, axis, [(i, i + by) for i in range(size) if 0 <= i + by < size])


def gathering(forcing, inflow, self_solve, greens, kept_cols, counts):
    source, green_row, solve = forcing[0], greens[0, 0], self_solve[0, 0]
    valid = jnp.arange(green_row.shape[0], dtype=jnp.int32) < counts[0, 0]
    incoming = inflow
    for section in range(lax.axis_size("slab")):
        if section > 0:
            arrived = shifted(trace, "slab", 1)
            incoming = jnp.where(lax.axis_index("slab") == 0, inflow, arrived)
        gathered = lax.all_gather(incoming, "row", axis=0)
        chosen = gathered[kept_cols[0, 0]]
        chosen = jnp.where(valid[:, None, None], chosen, jnp.zeros((), chosen.dtype))
        total = jnp.einsum("kij,kjw->iw", green_row, chosen, preferred_element_type=jnp.float32)
        coupled = (total + source.astype(jnp.float32)).astype(jnp.bfloat16)
        trace = jnp.dot(solve, coupled, preferred_element_type=jnp.float32).astype(jnp.bfloat16)
    return trace[None]


def shards(forcing, inflow, self_solve, greens, kept_cols, counts):
    rows, slots = lax.axis_size("row"), greens.shape[2]
    chips = rows // CORES
    if rows == chips * CORES and chips & (chips - 1) == 0 and 1 < chips and rows <= 2 * slots:
        return direct(forcing, inflow, self_solve, greens, kept_cols, counts)
    return gathering(forcing, inflow, self_solve, greens, kept_cols, counts)


def solution(mesh):
    placed = (
        P("slab", "row", None),
        P("row", None),
        P("slab", "row", None, None),
        P("slab", "row", None, None, None),
        P("slab", "row", None),
        P("slab", "row"),
    )
    return jax.shard_map(
        shards, mesh=mesh, in_specs=placed, out_specs=P("slab", "row", None), check_vma=False
    )
```

```python
import functools

import jax
import jax.numpy as jnp
from jax import lax
from jax.experimental import pallas as pl
from jax.experimental.pallas import tpu as pltpu
from jax.sharding import PartitionSpec as P

CORES = 2
VMEM_LIMIT = 48 * 2**20
LAST_LAST = (((1,), (1,)), ((), ()))
LAST_FIRST = (((1,), (0,)), ((), ()))
FIRST_LAST = (((0,), (1,)), ((), ()))
IN_VMEM = pl.BlockSpec(memory_space=pltpu.VMEM)
IN_SMEM = pl.BlockSpec(memory_space=pltpu.SMEM)
ANYWHERE = pl.BlockSpec(memory_space=pl.ANY)


def params():
    return pltpu.CompilerParams(vmem_limit_bytes=VMEM_LIMIT)


def step_of(order, chips):
    half = chips // 2
    return half + order // 2 if order % 2 == 0 else half - 1 - order // 2


def order_of(step, chips):
    half = chips // 2
    return jnp.where(step >= half, 2 * (step - half), 2 * (half - 1 - step) + 1)


def position_of(slot, chips, cols_ref):
    me = lax.axis_index("row")
    chip, core = me // CORES, me % CORES
    column = cols_ref[0, 0, slot]
    return jnp.where(column % CORES == core, 0, chips) + order_of(chip ^ (column // CORES), chips)


def place_kernel(chips, cols_ref, count_ref, greens_ref, solve_in, source_in, placed_ref, solve_ref, source_ref, sems):
    slots, positions = greens_ref.shape[2], placed_ref.shape[0]

    @pl.when(lax.axis_index("slab") == 0)
    def _():
        copies = [
            pltpu.make_async_copy(solve_in.at[0, 0], solve_ref, sems.at[slots]),
            pltpu.make_async_copy(source_in, source_ref, sems.at[slots + 1]),
        ]
        for copy in copies:
            copy.start()
        if positions > slots:
            placed_ref[...] = jnp.zeros_like(placed_ref)
        moves = []
        for slot in range(slots):
            position = position_of(slot, chips, cols_ref)
            move = pltpu.make_async_copy(greens_ref.at[0, 0, slot], placed_ref.at[position], sems.at[slot])
            used = slot < count_ref[0, 0]
            moves.append((used, move))
            pl.when(used)(move.start)
            if positions == slots:

                @pl.when(jnp.logical_not(used))
                def _():
                    placed_ref[position] = jnp.zeros(placed_ref.shape[1:], placed_ref.dtype)

        for used, move in moves:
            pl.when(used)(move.wait)
        for copy in copies:
            copy.wait()


def place(chips, cols, count, greens, solve, source):
    slots, rows, depth = greens.shape[2:]
    return pl.pallas_call(
        functools.partial(place_kernel, chips),
        out_shape=(
            pltpu.VMEM((chips * CORES, rows, depth), greens.dtype),
            pltpu.VMEM(solve.shape[2:], solve.dtype),
            pltpu.VMEM(source.shape, source.dtype),
        ),
        in_specs=[IN_SMEM] * 2 + [ANYWHERE] * 3,
        out_specs=(IN_VMEM,) * 3,
        scratch_shapes=[pltpu.SemaphoreType.DMA((slots + 2,))],
        compiler_params=params(),
        cost_estimate=pl.CostEstimate(flops=0, bytes_accessed=2 * greens.size * 2, transcendentals=0),
        name="place",
    )(cols, count, greens, solve, source)


def fold_kernel(section, chips, cols_ref, count_ref, greens_ref, solve_in, source_in, folded_ref, base_ref, held_ref, solve_ref, source_ref, sems):
    slots, positions = greens_ref.shape[2], folded_ref.shape[0]

    @pl.when(lax.axis_index("slab") == section)
    def _():
        copies = [
            pltpu.make_async_copy(greens_ref.at[0, 0, slot], held_ref.at[slot], sems.at[slot]) for slot in range(slots)
        ]
        early_copies = [
            pltpu.make_async_copy(solve_in.at[0, 0], solve_ref, sems.at[slots]),
            pltpu.make_async_copy(source_in, source_ref, sems.at[slots + 1]),
        ]
        for copy in early_copies + copies:
            copy.start()
        if positions > slots:
            folded_ref[...] = jnp.zeros_like(folded_ref)
        for copy in early_copies:
            copy.wait()
        base_ref[...] = lax.dot_general(source_ref[...], solve_ref[...], LAST_LAST, preferred_element_type=jnp.float32)
        for slot, copy in enumerate(copies):
            position = position_of(slot, chips, cols_ref)
            copy.wait()
            solved = lax.dot_general(held_ref[slot], solve_ref[...], FIRST_LAST, preferred_element_type=jnp.float32)
            used = slot < count_ref[0, 0]
            folded_ref[position] = jnp.where(used, solved, jnp.zeros_like(solved)).astype(folded_ref.dtype)


def fold(section, chips, cols, count, greens, solve, source):
    slots, rows, depth = greens.shape[2:]
    return pl.pallas_call(
        functools.partial(fold_kernel, section, chips),
        out_shape=(
            pltpu.VMEM((chips * CORES, depth, rows), greens.dtype),
            pltpu.VMEM(source.shape, jnp.float32),
        ),
        in_specs=[IN_SMEM] * 2 + [ANYWHERE] * 3,
        out_specs=(IN_VMEM,) * 2,
        scratch_shapes=[
            pltpu.VMEM((slots, rows, depth), greens.dtype),
            pltpu.VMEM(solve.shape[2:], solve.dtype),
            pltpu.VMEM(source.shape, source.dtype),
            pltpu.SemaphoreType.DMA((slots + 2,)),
        ],
        compiler_params=params(),
        cost_estimate=pl.CostEstimate(
            flops=2 * greens.size * rows, bytes_accessed=2 * greens.size * 2, transcendentals=0
        ),
        name="fold",
    )(cols, count, greens, solve, source)


def products(tiles, positions, placed_ref, folded, total):
    for tile, position in zip(tiles, positions):
        dims = LAST_FIRST if folded else LAST_LAST
        total += lax.dot_general(tile[...], placed_ref[position], dims, preferred_element_type=jnp.float32)
    return total


def early_kernel(section, positions, placed_ref, before_ref, *refs):
    tiles, total_ref = refs[:-1], refs[-1]

    @pl.when(lax.axis_index("slab") == section)
    def _():
        before = before_ref[...].astype(jnp.float32)
        total_ref[...] = products(tiles, positions, placed_ref, section > 0, before)


def early(section, positions, placed, before, tiles):
    return pl.pallas_call(
        functools.partial(early_kernel, section, positions),
        out_shape=pltpu.VMEM(before.shape, jnp.float32),
        in_specs=[IN_VMEM] * (2 + len(tiles)),
        out_specs=IN_VMEM,
        compiler_params=params(),
        name="early_tiles",
    )(placed, before, *tiles)


def late_kernel(section, position, placed_ref, total_ref, tile_ref, *refs):
    solve_ref, trace_ref = refs[0], refs[-1]

    @pl.when(lax.axis_index("slab") == section)
    def _():
        total = products([tile_ref], [position], placed_ref, section > 0, total_ref[...])
        if section == 0:
            coupled = total.astype(jnp.bfloat16)
            total = lax.dot_general(coupled, solve_ref[...], LAST_LAST, preferred_element_type=jnp.float32)
        trace_ref[...] = total.astype(trace_ref.dtype)


def late(section, position, placed, total, tile, solve, trace):
    operands = (placed, total, tile, solve, trace) if section == 0 else (placed, total, tile, trace)
    return pl.pallas_call(
        functools.partial(late_kernel, section, position),
        out_shape=pltpu.VMEM(trace.shape, trace.dtype),
        in_specs=[IN_VMEM] * len(operands),
        out_specs=IN_VMEM,
        input_output_aliases={len(operands) - 1: 0},
        compiler_params=params(),
        name="late_tile",
    )(*operands)


def swapped(tile, rows):
    return lax.ppermute(tile, "row", [(r, r ^ 1) for r in range(rows)])


def sent(tile, source, target, step, slabs, rows, via=None):
    pairs = [(source * rows + r, target * rows + (r ^ (step * CORES))) for r in range(rows)]
    busy = {source, target}
    if source != target and via is not None:
        pairs += [(target * rows + r, via * rows + (r if via != source else r ^ (step * CORES))) for r in range(rows)]
    if via not in (None, source):
        pairs += [(via * rows + r, source * rows + r) for r in range(rows)]
    if via is not None:
        busy.add(via)
        pairs += [(s * rows + r, s * rows + (r ^ 1)) for s in range(slabs) if s not in busy for r in range(rows)]
    return lax.ppermute(tile, ("slab", "row"), pairs)


def third_slabs(section, slabs, chips):
    free = [s % slabs for s in range(section + 1, section + slabs - 1)]
    free = [s for s in free if s != section - 2][-1:]
    return (free + [None] * chips)[:chips]


def direct(forcing, inflow, self_solve, greens, kept_cols, counts):
    slabs, rows = lax.axis_size("slab"), lax.axis_size("row")
    chips = rows // CORES
    steps = [step_of(order, chips) for order in range(chips)]
    entering, source = inflow.T, forcing[0].T
    greens, self_solve, source = (
        pltpu.with_memory_space_constraint(array, pltpu.HBM) for array in (greens, self_solve, source)
    )
    placed, solve, base = place(chips, kept_cols, counts, greens, self_solve, source)
    trace = jnp.zeros(entering.shape, jnp.bfloat16)
    for section in range(slabs):
        if section == 0:
            own = [sent(entering, 0, 0, step, slabs, rows, 0) for step in steps if step]
            entering, placed, base, solve, own[0] = lax.optimization_barrier((entering, placed, base, solve, own[0]))
            orders = [steps.index(0)] + [order for order, step in enumerate(steps) if step]
            own = [entering] + own
        else:
            vias = third_slabs(section, slabs, chips)
            own = [sent(trace, section - 1, section, step, slabs, rows, via) for step, via in zip(steps, vias)]
            orders = list(range(chips))
            placed, base = fold(section, chips, kept_cols, counts, greens, self_solve, source)
            placed, base, own[0] = lax.optimization_barrier((placed, base, own[0]))
        other = [swapped(tile, rows) for tile in own]
        arriving = []
        for order, *both in zip(orders, own, other):
            arriving += [(tile, side * chips + order) for side, tile in enumerate(both)]
        total = base
        for first in [0, *range(3, len(arriving) - 1, 2)]:
            tiles, positions = zip(*arriving[first : first + 3 if first == 0 else first + 2])
            total = early(section, positions, placed, total, tiles)
        trace = late(section, arriving[-1][1], placed, total, other[-1], solve, trace)
    return trace.T[None]


def shifted(array, axis, by):
    size = lax.axis_size(axis)
    return lax.ppermute(array, axis, [(i, i + by) for i in range(size) if 0 <= i + by < size])


def gathering(forcing, inflow, self_solve, greens, kept_cols, counts):
    source, green_row, solve = forcing[0], greens[0, 0], self_solve[0, 0]
    valid = jnp.arange(green_row.shape[0], dtype=jnp.int32) < counts[0, 0]
    incoming = inflow
    for section in range(lax.axis_size("slab")):
        if section > 0:
            arrived = shifted(trace, "slab", 1)
            incoming = jnp.where(lax.axis_index("slab") == 0, inflow, arrived)
        gathered = lax.all_gather(incoming, "row", axis=0)
        chosen = gathered[kept_cols[0, 0]]
        chosen = jnp.where(valid[:, None, None], chosen, jnp.zeros((), chosen.dtype))
        total = jnp.einsum("kij,kjw->iw", green_row, chosen, preferred_element_type=jnp.float32)
        coupled = (total + source.astype(jnp.float32)).astype(jnp.bfloat16)
        trace = jnp.dot(solve, coupled, preferred_element_type=jnp.float32).astype(jnp.bfloat16)
    return trace[None]


def shards(forcing, inflow, self_solve, greens, kept_cols, counts):
    rows, slots = lax.axis_size("row"), greens.shape[2]
    chips = rows // CORES
    if rows == chips * CORES and chips & (chips - 1) == 0 and 1 < chips and rows <= 2 * slots:
        return direct(forcing, inflow, self_solve, greens, kept_cols, counts)
    return gathering(forcing, inflow, self_solve, greens, kept_cols, counts)


def solution(mesh):
    placed = (
        P("slab", "row", None),
        P("row", None),
        P("slab", "row", None, None),
        P("slab", "row", None, None, None),
        P("slab", "row", None),
        P("slab", "row"),
    )
    return jax.shard_map(
        shards, mesh=mesh, in_specs=placed, out_specs=P("slab", "row", None), check_vma=False
    )
```

```python
import functools

import jax
import jax.numpy as jnp
from jax import lax
from jax.experimental import pallas as pl
from jax.experimental.pallas import tpu as pltpu
from jax.sharding import PartitionSpec as P

CORES = 2
VMEM_LIMIT = 48 * 2**20
LAST_LAST = (((1,), (1,)), ((), ()))
LAST_FIRST = (((1,), (0,)), ((), ()))
FIRST_LAST = (((0,), (1,)), ((), ()))
IN_VMEM = pl.BlockSpec(memory_space=pltpu.VMEM)
IN_SMEM = pl.BlockSpec(memory_space=pltpu.SMEM)
ANYWHERE = pl.BlockSpec(memory_space=pl.ANY)


def params():
    return pltpu.CompilerParams(vmem_limit_bytes=VMEM_LIMIT)


def step_of(order, chips):
    half = chips // 2
    return half + order // 2 if order % 2 == 0 else half - 1 - order // 2


def order_of(step, chips):
    half = chips // 2
    return jnp.where(step >= half, 2 * (step - half), 2 * (half - 1 - step) + 1)


def position_of(slot, chips, cols_ref):
    me = lax.axis_index("row")
    chip, core = me // CORES, me % CORES
    column = cols_ref[0, 0, slot]
    return jnp.where(column % CORES == core, 0, chips) + order_of(chip ^ (column // CORES), chips)


def place_kernel(chips, cols_ref, count_ref, greens_ref, solve_in, source_in, placed_ref, solve_ref, source_ref, sems):
    slots, positions = greens_ref.shape[2], placed_ref.shape[0]

    @pl.when(lax.axis_index("slab") == 0)
    def _():
        copies = [
            pltpu.make_async_copy(solve_in.at[0, 0], solve_ref, sems.at[slots]),
            pltpu.make_async_copy(source_in, source_ref, sems.at[slots + 1]),
        ]
        for copy in copies:
            copy.start()
        if positions > slots:
            placed_ref[...] = jnp.zeros_like(placed_ref)
        moves = []
        for slot in range(slots):
            position = position_of(slot, chips, cols_ref)
            move = pltpu.make_async_copy(greens_ref.at[0, 0, slot], placed_ref.at[position], sems.at[slot])
            used = slot < count_ref[0, 0]
            moves.append((used, move))
            pl.when(used)(move.start)
            if positions == slots:

                @pl.when(jnp.logical_not(used))
                def _():
                    placed_ref[position] = jnp.zeros(placed_ref.shape[1:], placed_ref.dtype)

        for used, move in moves:
            pl.when(used)(move.wait)
        for copy in copies:
            copy.wait()


def place(chips, cols, count, greens, solve, source):
    slots, rows, depth = greens.shape[2:]
    return pl.pallas_call(
        functools.partial(place_kernel, chips),
        out_shape=(
            pltpu.VMEM((chips * CORES, rows, depth), greens.dtype),
            pltpu.VMEM(solve.shape[2:], solve.dtype),
            pltpu.VMEM(source.shape, source.dtype),
        ),
        in_specs=[IN_SMEM] * 2 + [ANYWHERE] * 3,
        out_specs=(IN_VMEM,) * 3,
        scratch_shapes=[pltpu.SemaphoreType.DMA((slots + 2,))],
        compiler_params=params(),
        cost_estimate=pl.CostEstimate(flops=0, bytes_accessed=2 * greens.size * 2, transcendentals=0),
        name="place",
    )(cols, count, greens, solve, source)


def fold_kernel(section, chips, cols_ref, count_ref, greens_ref, solve_in, source_in, folded_ref, base_ref, held_ref, solve_ref, source_ref, sems):
    slots, positions = greens_ref.shape[2], folded_ref.shape[0]

    @pl.when(lax.axis_index("slab") == section)
    def _():
        copies = [
            pltpu.make_async_copy(greens_ref.at[0, 0, slot], held_ref.at[slot], sems.at[slot]) for slot in range(slots)
        ]
        early_copies = [
            pltpu.make_async_copy(solve_in.at[0, 0], solve_ref, sems.at[slots]),
            pltpu.make_async_copy(source_in, source_ref, sems.at[slots + 1]),
        ]
        for copy in early_copies + copies:
            copy.start()
        if positions > slots:
            folded_ref[...] = jnp.zeros_like(folded_ref)
        for copy in early_copies:
            copy.wait()
        base_ref[...] = lax.dot_general(source_ref[...], solve_ref[...], LAST_LAST, preferred_element_type=jnp.float32)
        for copy in copies:
            copy.wait()

        def fold_slot(slot, carry):
            solved = lax.dot_general(held_ref[slot], solve_ref[...], FIRST_LAST, preferred_element_type=jnp.float32)
            used = slot < count_ref[0, 0]
            solved = jnp.where(used, solved, jnp.zeros_like(solved)).astype(folded_ref.dtype)
            folded_ref[position_of(slot, chips, cols_ref)] = solved
            return carry

        lax.fori_loop(0, slots, fold_slot, 0)


def fold(section, chips, cols, count, greens, solve, source):
    slots, rows, depth = greens.shape[2:]
    return pl.pallas_call(
        functools.partial(fold_kernel, section, chips),
        out_shape=(
            pltpu.VMEM((chips * CORES, depth, rows), greens.dtype),
            pltpu.VMEM(source.shape, jnp.float32),
        ),
        in_specs=[IN_SMEM] * 2 + [ANYWHERE] * 3,
        out_specs=(IN_VMEM,) * 2,
        scratch_shapes=[
            pltpu.VMEM((slots, rows, depth), greens.dtype),
            pltpu.VMEM(solve.shape[2:], solve.dtype),
            pltpu.VMEM(source.shape, source.dtype),
            pltpu.SemaphoreType.DMA((slots + 2,)),
        ],
        compiler_params=params(),
        cost_estimate=pl.CostEstimate(
            flops=2 * greens.size * rows, bytes_accessed=2 * greens.size * 2, transcendentals=0
        ),
        name="fold",
    )(cols, count, greens, solve, source)


def products(tiles, positions, placed_ref, folded, total):
    for tile, position in zip(tiles, positions):
        dims = LAST_FIRST if folded else LAST_LAST
        total += lax.dot_general(tile[...], placed_ref[position], dims, preferred_element_type=jnp.float32)
    return total


def early_kernel(section, positions, placed_ref, before_ref, *refs):
    tiles, total_ref = refs[:-1], refs[-1]

    @pl.when(lax.axis_index("slab") == section)
    def _():
        before = before_ref[...].astype(jnp.float32)
        total_ref[...] = products(tiles, positions, placed_ref, section > 0, before)


def early(section, positions, placed, before, tiles):
    return pl.pallas_call(
        functools.partial(early_kernel, section, positions),
        out_shape=pltpu.VMEM(before.shape, jnp.float32),
        in_specs=[IN_VMEM] * (2 + len(tiles)),
        out_specs=IN_VMEM,
        compiler_params=params(),
        name="early_tiles",
    )(placed, before, *tiles)


def late_kernel(section, position, placed_ref, total_ref, tile_ref, *refs):
    solve_ref, trace_ref = refs[0], refs[-1]

    @pl.when(lax.axis_index("slab") == section)
    def _():
        total = products([tile_ref], [position], placed_ref, section > 0, total_ref[...])
        if section == 0:
            coupled = total.astype(jnp.bfloat16)
            total = lax.dot_general(coupled, solve_ref[...], LAST_LAST, preferred_element_type=jnp.float32)
        trace_ref[...] = total.astype(trace_ref.dtype)


def late(section, position, placed, total, tile, solve, trace):
    operands = (placed, total, tile, solve, trace) if section == 0 else (placed, total, tile, trace)
    return pl.pallas_call(
        functools.partial(late_kernel, section, position),
        out_shape=pltpu.VMEM(trace.shape, trace.dtype),
        in_specs=[IN_VMEM] * len(operands),
        out_specs=IN_VMEM,
        input_output_aliases={len(operands) - 1: 0},
        compiler_params=params(),
        name="late_tile",
    )(*operands)


def swapped(tile, rows):
    return lax.ppermute(tile, "row", [(r, r ^ 1) for r in range(rows)])


def sent(tile, source, target, step, slabs, rows, via):
    partner = [r ^ (step * CORES) for r in range(rows)]
    pairs = [(source * rows + r, target * rows + partner[r]) for r in range(rows)]
    if via is not None:
        path = [target, *via, source] if source != target else [source]
        for here, there in zip(path, path[1:]):
            pairs += [(here * rows + r, there * rows + (r if via else partner[r])) for r in range(rows)]
        pairs += [(s * rows + r, s * rows + (r ^ 1)) for s in range(slabs) if s not in path for r in range(rows)]
    return lax.ppermute(tile, ("slab", "row"), pairs)


def ways(section, slabs, chips):
    others = [s % slabs for s in range(section + 1, section + slabs - 1)]
    if len(others) < 2 or chips < 4:
        return [None] * chips
    free, late = others[0], others[-1]
    if section == 1:
        return [(free,), None, None, None] + [None] * (chips - 4)
    if section < slabs - 1:
        return [(free,), None, None, None] + [None] * (chips - 4)
    return [(free,), None, (late, free), ()][:1] + [None] * (chips - 4) + [(free,), None, (late, free), ()][1:]


def direct(forcing, inflow, self_solve, greens, kept_cols, counts):
    slabs, rows = lax.axis_size("slab"), lax.axis_size("row")
    chips, last = rows // CORES, slabs - 1
    steps = [step_of(order, chips) for order in range(chips)]
    entering, source = inflow.T, forcing[0].T
    greens, self_solve, source = (
        pltpu.with_memory_space_constraint(array, pltpu.HBM) for array in (greens, self_solve, source)
    )
    given = (chips, kept_cols, counts, greens, self_solve, source)
    placed, solve, base = place(*given)
    ready = fold(last, *given) if last > 0 else ()
    trace = jnp.zeros(entering.shape, jnp.bfloat16)
    for section in range(slabs):
        if section == 0:
            own = [sent(entering, 0, 0, step, slabs, rows, ()) for step in steps if step]
            placed, base, solve, *ready, own[0] = lax.optimization_barrier((placed, base, solve, *ready, own[0]))
            orders = [steps.index(0)] + [order for order, step in enumerate(steps) if step]
            own = [entering] + own
        else:
            vias = ways(section, slabs, chips)
            own = [sent(trace, section - 1, section, step, slabs, rows, via) for step, via in zip(steps, vias)]
            orders = list(range(chips))
            if section < last:
                placed, base = fold(section, *given)
                placed, base, own[0] = lax.optimization_barrier((placed, base, own[0]))
            else:
                placed, base = ready
        other = [swapped(tile, rows) for tile in own]
        arriving = []
        for order, *both in zip(orders, own, other):
            arriving += [(tile, side * chips + order) for side, tile in enumerate(both)]
        total = base
        for first in [0, *range(3, len(arriving) - 1, 2)]:
            tiles, positions = zip(*arriving[first : first + 3 if first == 0 else first + 2])
            total = early(section, positions, placed, total, tiles)
        trace = late(section, arriving[-1][1], placed, total, other[-1], solve, trace)
    return trace.T[None]


def shifted(array, axis, by):
    size = lax.axis_size(axis)
    return lax.ppermute(array, axis, [(i, i + by) for i in range(size) if 0 <= i + by < size])


def gathering(forcing, inflow, self_solve, greens, kept_cols, counts):
    source, green_row, solve = forcing[0], greens[0, 0], self_solve[0, 0]
    valid = jnp.arange(green_row.shape[0], dtype=jnp.int32) < counts[0, 0]
    incoming = inflow
    for section in range(lax.axis_size("slab")):
        if section > 0:
            arrived = shifted(trace, "slab", 1)
            incoming = jnp.where(lax.axis_index("slab") == 0, inflow, arrived)
        gathered = lax.all_gather(incoming, "row", axis=0)
        chosen = gathered[kept_cols[0, 0]]
        chosen = jnp.where(valid[:, None, None], chosen, jnp.zeros((), chosen.dtype))
        total = jnp.einsum("kij,kjw->iw", green_row, chosen, preferred_element_type=jnp.float32)
        coupled = (total + source.astype(jnp.float32)).astype(jnp.bfloat16)
        trace = jnp.dot(solve, coupled, preferred_element_type=jnp.float32).astype(jnp.bfloat16)
    return trace[None]


def shards(forcing, inflow, self_solve, greens, kept_cols, counts):
    rows, slots = lax.axis_size("row"), greens.shape[2]
    chips = rows // CORES
    if rows == chips * CORES and chips & (chips - 1) == 0 and 1 < chips and rows <= 2 * slots:
        return direct(forcing, inflow, self_solve, greens, kept_cols, counts)
    return gathering(forcing, inflow, self_solve, greens, kept_cols, counts)


def solution(mesh):
    placed = (
        P("slab", "row", None),
        P("row", None),
        P("slab", "row", None, None),
        P("slab", "row", None, None, None),
        P("slab", "row", None),
        P("slab", "row"),
    )
    return jax.shard_map(
        shards, mesh=mesh, in_specs=placed, out_specs=P("slab", "row", None), check_vma=False
    )
```

```python
import functools

import jax
import jax.numpy as jnp
from jax import lax
from jax.experimental import pallas as pl
from jax.experimental.pallas import tpu as pltpu
from jax.sharding import PartitionSpec as P

CORES = 2
VMEM_LIMIT = 48 * 2**20
LAST_LAST = (((1,), (1,)), ((), ()))
LAST_FIRST = (((1,), (0,)), ((), ()))
FIRST_LAST = (((0,), (1,)), ((), ()))
IN_VMEM = pl.BlockSpec(memory_space=pltpu.VMEM)
IN_SMEM = pl.BlockSpec(memory_space=pltpu.SMEM)
ANYWHERE = pl.BlockSpec(memory_space=pl.ANY)


def params():
    return pltpu.CompilerParams(vmem_limit_bytes=VMEM_LIMIT)


def step_of(order, chips):
    half = chips // 2
    return half + order // 2 if order % 2 == 0 else half - 1 - order // 2


def order_of(step, chips):
    half = chips // 2
    return jnp.where(step >= half, 2 * (step - half), 2 * (half - 1 - step) + 1)


def position_of(slot, chips, cols_ref):
    me = lax.axis_index("row")
    chip, core = me // CORES, me % CORES
    column = cols_ref[0, 0, slot]
    return jnp.where(column % CORES == core, 0, chips) + order_of(chip ^ (column // CORES), chips)


def spot_of(spots_ref, slot, positions):
    spot = spots_ref[slot]
    return spot < positions, jnp.where(spot < positions, spot, spot - positions)


def place_kernel(chips, cols_ref, count_ref, greens_ref, solve_in, source_in, spots_ref, placed_ref, solve_ref, source_ref, sems):
    slots, positions = greens_ref.shape[2], placed_ref.shape[0]
    for slot in range(slots):
        position = position_of(slot, chips, cols_ref)
        spots_ref[slot] = jnp.where(slot < count_ref[0, 0], position, position + positions)

    @pl.when(lax.axis_index("slab") == 0)
    def _():
        copies = [
            pltpu.make_async_copy(solve_in.at[0, 0], solve_ref, sems.at[slots]),
            pltpu.make_async_copy(source_in, source_ref, sems.at[slots + 1]),
        ]
        for copy in copies:
            copy.start()
        if positions > slots:
            placed_ref[...] = jnp.zeros_like(placed_ref)
        moves = []
        for slot in range(slots):
            used, position = spot_of(spots_ref, slot, positions)
            move = pltpu.make_async_copy(greens_ref.at[0, 0, slot], placed_ref.at[position], sems.at[slot])
            moves.append((used, move))
            pl.when(used)(move.start)
            if positions == slots:

                @pl.when(jnp.logical_not(used))
                def _():
                    placed_ref[position] = jnp.zeros(placed_ref.shape[1:], placed_ref.dtype)

        for used, move in moves:
            pl.when(used)(move.wait)
        for copy in copies:
            copy.wait()


def place(chips, cols, count, greens, solve, source):
    slots, rows, depth = greens.shape[2:]
    return pl.pallas_call(
        functools.partial(place_kernel, chips),
        out_shape=(
            pltpu.SMEM((slots,), jnp.int32),
            pltpu.VMEM((chips * CORES, rows, depth), greens.dtype),
            pltpu.VMEM(solve.shape[2:], solve.dtype),
            pltpu.VMEM(source.shape, source.dtype),
        ),
        in_specs=[IN_SMEM] * 2 + [ANYWHERE] * 3,
        out_specs=(IN_SMEM,) + (IN_VMEM,) * 3,
        scratch_shapes=[pltpu.SemaphoreType.DMA((slots + 2,))],
        compiler_params=params(),
        cost_estimate=pl.CostEstimate(flops=0, bytes_accessed=2 * greens.size * 2, transcendentals=0),
        name="place",
    )(cols, count, greens, solve, source)


def fold_kernel(section, spots_ref, greens_ref, solve_in, source_in, folded_ref, base_ref, held_ref, solve_ref, source_ref, sems):
    slots, positions = greens_ref.shape[2], folded_ref.shape[0]

    @pl.when(lax.axis_index("slab") == section)
    def _():
        copies = [
            pltpu.make_async_copy(solve_in.at[0, 0], solve_ref, sems.at[slots]),
            pltpu.make_async_copy(source_in, source_ref, sems.at[slots + 1]),
        ]
        copies += [
            pltpu.make_async_copy(greens_ref.at[0, 0, slot], held_ref.at[slot], sems.at[slot]) for slot in range(slots)
        ]
        for copy in copies:
            copy.start()
        if positions > slots:
            folded_ref[...] = jnp.zeros_like(folded_ref)
        for copy in copies:
            copy.wait()
        base_ref[...] = lax.dot_general(source_ref[...], solve_ref[...], LAST_LAST, preferred_element_type=jnp.float32)

        def fold_slot(slot, carry):
            solved = lax.dot_general(held_ref[slot], solve_ref[...], FIRST_LAST, preferred_element_type=jnp.float32)
            used, position = spot_of(spots_ref, slot, positions)
            folded_ref[position] = jnp.where(used, solved, jnp.zeros_like(solved)).astype(folded_ref.dtype)
            return carry

        lax.fori_loop(0, slots, fold_slot, 0)


def fold(section, positions, spots, greens, solve, source):
    slots, rows, depth = greens.shape[2:]
    return pl.pallas_call(
        functools.partial(fold_kernel, section),
        out_shape=(
            pltpu.VMEM((positions, depth, rows), greens.dtype),
            pltpu.VMEM(source.shape, jnp.float32),
        ),
        in_specs=[IN_SMEM] + [ANYWHERE] * 3,
        out_specs=(IN_VMEM,) * 2,
        scratch_shapes=[
            pltpu.VMEM((slots, rows, depth), greens.dtype),
            pltpu.VMEM(solve.shape[2:], solve.dtype),
            pltpu.VMEM(source.shape, source.dtype),
            pltpu.SemaphoreType.DMA((slots + 2,)),
        ],
        compiler_params=params(),
        cost_estimate=pl.CostEstimate(
            flops=2 * greens.size * rows, bytes_accessed=2 * greens.size * 2, transcendentals=0
        ),
        name="fold",
    )(spots, greens, solve, source)


def products(tiles, positions, placed_ref, folded, total):
    for tile, position in zip(tiles, positions):
        dims = LAST_FIRST if folded else LAST_LAST
        total += lax.dot_general(tile[...], placed_ref[position], dims, preferred_element_type=jnp.float32)
    return total


def early_kernel(section, positions, placed_ref, before_ref, *refs):
    tiles, total_ref = refs[:-1], refs[-1]

    @pl.when(lax.axis_index("slab") == section)
    def _():
        before = before_ref[...].astype(jnp.float32)
        total_ref[...] = products(tiles, positions, placed_ref, section > 0, before)


def early(section, positions, placed, before, tiles):
    return pl.pallas_call(
        functools.partial(early_kernel, section, positions),
        out_shape=pltpu.VMEM(before.shape, jnp.float32),
        in_specs=[IN_VMEM] * (2 + len(tiles)),
        out_specs=IN_VMEM,
        compiler_params=params(),
        name="early_tiles",
    )(placed, before, *tiles)


def late_kernel(section, position, placed_ref, total_ref, tile_ref, *refs):
    solve_ref, trace_ref = refs[0], refs[-1]

    @pl.when(lax.axis_index("slab") == section)
    def _():
        total = products([tile_ref], [position], placed_ref, section > 0, total_ref[...])
        if section == 0:
            coupled = total.astype(jnp.bfloat16)
            total = lax.dot_general(coupled, solve_ref[...], LAST_LAST, preferred_element_type=jnp.float32)
        trace_ref[...] = total.astype(trace_ref.dtype)


def late(section, position, placed, total, tile, solve, trace):
    operands = (placed, total, tile, solve, trace) if section == 0 else (placed, total, tile, trace)
    return pl.pallas_call(
        functools.partial(late_kernel, section, position),
        out_shape=pltpu.VMEM(trace.shape, trace.dtype),
        in_specs=[IN_VMEM] * len(operands),
        out_specs=IN_VMEM,
        input_output_aliases={len(operands) - 1: 0},
        compiler_params=params(),
        name="late_tile",
    )(*operands)


def swapped(tile, rows):
    return lax.ppermute(tile, "row", [(r, r ^ 1) for r in range(rows)])


def sent(tile, source, target, step, slabs, rows, via):
    partner = [r ^ (step * CORES) for r in range(rows)]
    pairs = [(source * rows + r, target * rows + partner[r]) for r in range(rows)]
    if via is not None:
        path = [target, *via, source] if source != target else [source]
        for here, there in zip(path, path[1:]):
            pairs += [(here * rows + r, there * rows + (r if via else partner[r])) for r in range(rows)]
        pairs += [(s * rows + r, s * rows + (r ^ 1)) for s in range(slabs) if s not in path for r in range(rows)]
    return lax.ppermute(tile, ("slab", "row"), pairs)


def ways(section, slabs, chips):
    others = [s % slabs for s in range(section + 1, section + slabs - 1)]
    if len(others) < 2 or chips < 4:
        return [None] * chips
    free, late = others[0], others[-1]
    if section < slabs - 1:
        return [(free,)] + [None] * (chips - 1)
    return [(free,)] + [None] * (chips - 3) + [(late, free), ()]


def direct(forcing, inflow, self_solve, greens, kept_cols, counts):
    slabs, rows = lax.axis_size("slab"), lax.axis_size("row")
    chips, last = rows // CORES, slabs - 1
    steps = [step_of(order, chips) for order in range(chips)]
    entering, source = inflow.T, forcing[0].T
    greens, self_solve, source = (
        pltpu.with_memory_space_constraint(array, pltpu.HBM) for array in (greens, self_solve, source)
    )
    spots, placed, solve, base = place(chips, kept_cols, counts, greens, self_solve, source)
    given = (rows, spots, greens, self_solve, source)
    ready = fold(last, *given) if last > 0 else ()
    trace = jnp.zeros(entering.shape, jnp.bfloat16)
    for section in range(slabs):
        if section == 0:
            own = [sent(entering, 0, 0, step, slabs, rows, ()) for step in steps if step]
            placed, base, solve, *ready, own[0] = lax.optimization_barrier((placed, base, solve, *ready, own[0]))
            orders = [steps.index(0)] + [order for order, step in enumerate(steps) if step]
            own = [entering] + own
        else:
            vias = ways(section, slabs, chips)
            own = [sent(trace, section - 1, section, step, slabs, rows, via) for step, via in zip(steps, vias)]
            orders = list(range(chips))
            if section < last:
                placed, base = fold(section, *given)
                placed, base, own[0] = lax.optimization_barrier((placed, base, own[0]))
            else:
                placed, base = ready
        if section == 0:
            other = [swapped(tile, rows) for tile in own[:-1]]
            held = [(own[0], orders[0]), (other[0], chips + orders[0])] + [(own[i], orders[i]) for i in range(1, chips - 1)]
            tiles, positions = zip(*held)
            total = early(section, positions, placed, base, tiles)
            own[-1], total = lax.optimization_barrier((own[-1], total))
            other.append(swapped(own[-1], rows))
            held = [(other[i], chips + orders[i]) for i in range(1, chips - 1)] + [(own[-1], orders[-1])]
            tiles, positions = zip(*held)
            total = early(section, positions, placed, total, tiles)
            arriving = [(None, chips + orders[-1])]
        else:
            other = [swapped(tile, rows) for tile in own]
            arriving = []
            for order, *both in zip(orders, own, other):
                arriving += [(tile, side * chips + order) for side, tile in enumerate(both)]
            total = base
            for first in [0, *range(3, len(arriving) - 1, 2)]:
                tiles, positions = zip(*arriving[first : first + 3 if first == 0 else first + 2])
                total = early(section, positions, placed, total, tiles)
        trace = late(section, arriving[-1][1], placed, total, other[-1], solve, trace)
    return trace.T[None]


def shifted(array, axis, by):
    size = lax.axis_size(axis)
    return lax.ppermute(array, axis, [(i, i + by) for i in range(size) if 0 <= i + by < size])


def gathering(forcing, inflow, self_solve, greens, kept_cols, counts):
    source, green_row, solve = forcing[0], greens[0, 0], self_solve[0, 0]
    valid = jnp.arange(green_row.shape[0], dtype=jnp.int32) < counts[0, 0]
    incoming = inflow
    for section in range(lax.axis_size("slab")):
        if section > 0:
            arrived = shifted(trace, "slab", 1)
            incoming = jnp.where(lax.axis_index("slab") == 0, inflow, arrived)
        gathered = lax.all_gather(incoming, "row", axis=0)
        chosen = gathered[kept_cols[0, 0]]
        chosen = jnp.where(valid[:, None, None], chosen, jnp.zeros((), chosen.dtype))
        total = jnp.einsum("kij,kjw->iw", green_row, chosen, preferred_element_type=jnp.float32)
        coupled = (total + source.astype(jnp.float32)).astype(jnp.bfloat16)
        trace = jnp.dot(solve, coupled, preferred_element_type=jnp.float32).astype(jnp.bfloat16)
    return trace[None]


def shards(forcing, inflow, self_solve, greens, kept_cols, counts):
    rows, slots = lax.axis_size("row"), greens.shape[2]
    chips = rows // CORES
    if rows == chips * CORES and chips & (chips - 1) == 0 and 1 < chips and rows <= 2 * slots:
        return direct(forcing, inflow, self_solve, greens, kept_cols, counts)
    return gathering(forcing, inflow, self_solve, greens, kept_cols, counts)


def solution(mesh):
    placed = (
        P("slab", "row", None),
        P("row", None),
        P("slab", "row", None, None),
        P("slab", "row", None, None, None),
        P("slab", "row", None),
        P("slab", "row"),
    )
    return jax.shard_map(
        shards, mesh=mesh, in_specs=placed, out_specs=P("slab", "row", None), check_vma=False
    )
```

```python
import functools

import jax
import jax.numpy as jnp
from jax import lax
from jax.experimental import pallas as pl
from jax.experimental.pallas import tpu as pltpu
from jax.sharding import PartitionSpec as P

CORES = 2
VMEM_LIMIT = 48 * 2**20
LAST_LAST = (((1,), (1,)), ((), ()))
LAST_FIRST = (((1,), (0,)), ((), ()))
FIRST_LAST = (((0,), (1,)), ((), ()))
IN_VMEM = pl.BlockSpec(memory_space=pltpu.VMEM)
IN_SMEM = pl.BlockSpec(memory_space=pltpu.SMEM)
ANYWHERE = pl.BlockSpec(memory_space=pl.ANY)


def params():
    return pltpu.CompilerParams(vmem_limit_bytes=VMEM_LIMIT)


def step_of(order, chips):
    half = chips // 2
    return half + order // 2 if order % 2 == 0 else half - 1 - order // 2


def order_of(step, chips):
    half = chips // 2
    return jnp.where(step >= half, 2 * (step - half), 2 * (half - 1 - step) + 1)


def position_of(slot, chips, cols_ref):
    me = lax.axis_index("row")
    chip, core = me // CORES, me % CORES
    column = cols_ref[0, 0, slot]
    return jnp.where(column % CORES == core, 0, chips) + order_of(chip ^ (column // CORES), chips)


def spot_of(spots_ref, slot, positions):
    spot = spots_ref[slot]
    return spot < positions, jnp.where(spot < positions, spot, spot - positions)


def place_kernel(chips, cols_in, count_ref, greens_ref, solve_in, source_in, *refs):
    spots_ref, slots_ref, held_ref, solve_ref, source_ref, cols_ref, sems = refs
    slots, positions = greens_ref.shape[2], slots_ref.shape[0]
    table = pltpu.make_async_copy(cols_in, cols_ref, sems.at[0])
    copies = [
        pltpu.make_async_copy(greens_ref.at[0, 0], held_ref, sems.at[1]),
        pltpu.make_async_copy(solve_in.at[0, 0], solve_ref, sems.at[2]),
        pltpu.make_async_copy(source_in, source_ref, sems.at[3]),
    ]
    first = lax.axis_index("slab") == 0
    table.start()

    @pl.when(first)
    def _():
        for copy in copies:
            copy.start()

    for position in range(positions):
        slots_ref[position] = -1
    table.wait()
    for slot in range(slots):
        position, used = position_of(slot, chips, cols_ref), slot < count_ref[0, 0]
        spots_ref[slot] = jnp.where(used, position, position + positions)

        @pl.when(used)
        def _():
            slots_ref[position] = slot

    @pl.when(first)
    def _():
        for copy in copies:
            copy.wait()


def place(chips, cols, count, greens, solve, source):
    slots, rows, depth = greens.shape[2:]
    return pl.pallas_call(
        functools.partial(place_kernel, chips),
        out_shape=(
            pltpu.SMEM((slots,), jnp.int32),
            pltpu.SMEM((chips * CORES,), jnp.int32),
            pltpu.VMEM((slots, rows, depth), greens.dtype),
            pltpu.VMEM(solve.shape[2:], solve.dtype),
            pltpu.VMEM(source.shape, source.dtype),
        ),
        in_specs=[ANYWHERE, IN_SMEM] + [ANYWHERE] * 3,
        out_specs=(IN_SMEM,) * 2 + (IN_VMEM,) * 3,
        scratch_shapes=[
            pltpu.SMEM(cols.shape, cols.dtype),
            pltpu.SemaphoreType.DMA((4,)),
        ],
        compiler_params=params(),
        cost_estimate=pl.CostEstimate(flops=0, bytes_accessed=2 * greens.size * 2, transcendentals=0),
        name="place",
    )(cols, count, greens, solve, source)


def fold_kernel(section, spots_ref, greens_ref, solve_in, source_in, folded_ref, base_ref, held_ref, solve_ref, source_ref, sems):
    slots, positions = greens_ref.shape[2], folded_ref.shape[0]

    @pl.when(lax.axis_index("slab") == section)
    def _():
        copies = [
            pltpu.make_async_copy(solve_in.at[0, 0], solve_ref, sems.at[slots]),
            pltpu.make_async_copy(source_in, source_ref, sems.at[slots + 1]),
        ]
        copies += [
            pltpu.make_async_copy(greens_ref.at[0, 0, slot], held_ref.at[slot], sems.at[slot]) for slot in range(slots)
        ]
        for copy in copies:
            copy.start()
        if positions > slots:
            folded_ref[...] = jnp.zeros_like(folded_ref)
        for copy in copies:
            copy.wait()
        base_ref[...] = lax.dot_general(source_ref[...], solve_ref[...], LAST_LAST, preferred_element_type=jnp.float32)

        def fold_slot(slot, carry):
            solved = lax.dot_general(held_ref[slot], solve_ref[...], FIRST_LAST, preferred_element_type=jnp.float32)
            used, position = spot_of(spots_ref, slot, positions)
            folded_ref[position] = jnp.where(used, solved, jnp.zeros_like(solved)).astype(folded_ref.dtype)
            return carry

        lax.fori_loop(0, slots, fold_slot, 0)


def fold(section, positions, spots, greens, solve, source):
    slots, rows, depth = greens.shape[2:]
    return pl.pallas_call(
        functools.partial(fold_kernel, section),
        out_shape=(
            pltpu.VMEM((positions, depth, rows), greens.dtype),
            pltpu.VMEM(source.shape, jnp.float32),
        ),
        in_specs=[IN_SMEM] + [ANYWHERE] * 3,
        out_specs=(IN_VMEM,) * 2,
        scratch_shapes=[
            pltpu.VMEM((slots, rows, depth), greens.dtype),
            pltpu.VMEM(solve.shape[2:], solve.dtype),
            pltpu.VMEM(source.shape, source.dtype),
            pltpu.SemaphoreType.DMA((slots + 2,)),
        ],
        compiler_params=params(),
        cost_estimate=pl.CostEstimate(
            flops=2 * greens.size * rows, bytes_accessed=2 * greens.size * 2, transcendentals=0
        ),
        name="fold",
    )(spots, greens, solve, source)


def products(tiles, positions, placed_ref, slots_ref, total):
    for tile, position in zip(tiles, positions):
        if slots_ref is None:
            total += jnp.dot(tile[...], placed_ref[position], preferred_element_type=jnp.float32)
        else:
            slot = slots_ref[position]
            used = jnp.where(slot >= 0, tile[...], jnp.zeros_like(tile))
            total += lax.dot_general(
                used, placed_ref[jnp.maximum(slot, 0)], LAST_LAST, preferred_element_type=jnp.float32
            )
    return total


def early_kernel(section, positions, *refs):
    slots_ref, refs = (refs[0], refs[1:]) if section == 0 else (None, refs)
    placed_ref, before_ref, tiles, total_ref = refs[0], refs[1], refs[2:-1], refs[-1]

    @pl.when(lax.axis_index("slab") == section)
    def _():
        before = before_ref[...].astype(jnp.float32)
        total_ref[...] = products(tiles, positions, placed_ref, slots_ref, before)


def early(section, positions, slots, placed, before, tiles):
    scalars = [slots] if section == 0 else []
    return pl.pallas_call(
        functools.partial(early_kernel, section, positions),
        out_shape=pltpu.VMEM(before.shape, jnp.float32),
        in_specs=[IN_SMEM] * len(scalars) + [IN_VMEM] * (2 + len(tiles)),
        out_specs=IN_VMEM,
        compiler_params=params(),
        name="early_tiles",
    )(*scalars, placed, before, *tiles)


def late_kernel(section, position, *refs):
    slots_ref, refs = (refs[0], refs[1:]) if section == 0 else (None, refs)
    placed_ref, total_ref, tile_ref, solve_ref, trace_ref = *refs[:3], refs[3], refs[-1]

    @pl.when(lax.axis_index("slab") == section)
    def _():
        total = products([tile_ref], [position], placed_ref, slots_ref, total_ref[...])
        if section == 0:
            coupled = total.astype(jnp.bfloat16)
            total = lax.dot_general(coupled, solve_ref[...], LAST_LAST, preferred_element_type=jnp.float32)
        trace_ref[...] = total.astype(trace_ref.dtype)


def late(section, position, slots, placed, total, tile, solve, trace):
    scalars = [slots] if section == 0 else []
    operands = [placed, total, tile, *([solve] if section == 0 else []), trace]
    return pl.pallas_call(
        functools.partial(late_kernel, section, position),
        out_shape=pltpu.VMEM(trace.shape, trace.dtype),
        in_specs=[IN_SMEM] * len(scalars) + [IN_VMEM] * len(operands),
        out_specs=IN_VMEM,
        input_output_aliases={len(scalars) + len(operands) - 1: 0},
        compiler_params=params(),
        name="late_tile",
    )(*scalars, *operands)


def swapped(tile, rows):
    return lax.ppermute(tile, "row", [(r, r ^ 1) for r in range(rows)])


def sent(tile, source, target, step, slabs, rows, via):
    partner = [r ^ (step * CORES) for r in range(rows)]
    pairs = [(source * rows + r, target * rows + partner[r]) for r in range(rows)]
    if via is not None:
        path = [target, *via, source] if source != target else [source]
        for here, there in zip(path, path[1:]):
            pairs += [(here * rows + r, there * rows + (r if via else partner[r])) for r in range(rows)]
        pairs += [(s * rows + r, s * rows + (r ^ 1)) for s in range(slabs) if s not in path for r in range(rows)]
    return lax.ppermute(tile, ("slab", "row"), pairs)


def ways(section, slabs, chips):
    others = [s % slabs for s in range(section + 1, section + slabs - 1)]
    if len(others) < 2 or chips < 4:
        return [None] * chips
    free, late = others[0], others[-1]
    if section < slabs - 1:
        return [(free,)] + [None] * (chips - 1)
    return [(free,)] + [None] * (chips - 3) + [(late, free), ()]


def direct(forcing, inflow, self_solve, greens, kept_cols, counts):
    slabs, rows = lax.axis_size("slab"), lax.axis_size("row")
    chips, last = rows // CORES, slabs - 1
    steps = [step_of(order, chips) for order in range(chips)]
    entering, source = inflow.T, forcing[0].T
    kept_cols, greens, self_solve, source = (
        pltpu.with_memory_space_constraint(array, pltpu.HBM) for array in (kept_cols, greens, self_solve, source)
    )
    spots, slots, placed, solve, base = place(chips, kept_cols, counts, greens, self_solve, source)
    given = (rows, spots, greens, self_solve, source)
    ready = fold(last, *given) if last > 0 else ()
    trace = jnp.zeros(entering.shape, jnp.bfloat16)
    for section in range(slabs):
        if section == 0:
            own = [sent(entering, 0, 0, step, slabs, rows, ()) for step in steps if step]
            placed, base, solve, *ready, own[0] = lax.optimization_barrier((placed, base, solve, *ready, own[0]))
            orders = [steps.index(0)] + [order for order, step in enumerate(steps) if step]
            own = [entering] + own
        else:
            vias = ways(section, slabs, chips)
            own = [sent(trace, section - 1, section, step, slabs, rows, via) for step, via in zip(steps, vias)]
            orders = list(range(chips))
            if section < last:
                placed, base = fold(section, *given)
                placed, base, own[0] = lax.optimization_barrier((placed, base, own[0]))
            else:
                placed, base = ready
        if section == 0:
            other = [swapped(tile, rows) for tile in own[:-1]]
            held = [(own[0], orders[0]), (other[0], chips + orders[0])]
            tiles, positions = zip(*held)
            total = early(section, positions, slots, placed, base, tiles)
            own[1], total = lax.optimization_barrier((own[1], total))
            other.append(swapped(own[-1], rows))
            held = [(own[i], orders[i]) for i in range(1, chips)] + [(other[i], chips + orders[i]) for i in range(1, chips - 1)]
            tiles, positions = zip(*held)
            total = early(section, positions, slots, placed, total, tiles)
            arriving = [(None, chips + orders[-1])]
        else:
            other = [swapped(tile, rows) for tile in own]
            arriving = []
            for order, *both in zip(orders, own, other):
                arriving += [(tile, side * chips + order) for side, tile in enumerate(both)]
            total = base
            for first in [0, *range(3, len(arriving) - 1, 2)]:
                tiles, positions = zip(*arriving[first : first + 3 if first == 0 else first + 2])
                total = early(section, positions, slots, placed, total, tiles)
        trace = late(section, arriving[-1][1], slots, placed, total, other[-1], solve, trace)
    return trace.T[None]


def shifted(array, axis, by):
    size = lax.axis_size(axis)
    return lax.ppermute(array, axis, [(i, i + by) for i in range(size) if 0 <= i + by < size])


def gathering(forcing, inflow, self_solve, greens, kept_cols, counts):
    source, green_row, solve = forcing[0], greens[0, 0], self_solve[0, 0]
    valid = jnp.arange(green_row.shape[0], dtype=jnp.int32) < counts[0, 0]
    incoming = inflow
    for section in range(lax.axis_size("slab")):
        if section > 0:
            arrived = shifted(trace, "slab", 1)
            incoming = jnp.where(lax.axis_index("slab") == 0, inflow, arrived)
        gathered = lax.all_gather(incoming, "row", axis=0)
        chosen = gathered[kept_cols[0, 0]]
        chosen = jnp.where(valid[:, None, None], chosen, jnp.zeros((), chosen.dtype))
        total = jnp.einsum("kij,kjw->iw", green_row, chosen, preferred_element_type=jnp.float32)
        coupled = (total + source.astype(jnp.float32)).astype(jnp.bfloat16)
        trace = jnp.dot(solve, coupled, preferred_element_type=jnp.float32).astype(jnp.bfloat16)
    return trace[None]


def shards(forcing, inflow, self_solve, greens, kept_cols, counts):
    rows, slots = lax.axis_size("row"), greens.shape[2]
    chips = rows // CORES
    if rows == chips * CORES and chips & (chips - 1) == 0 and 1 < chips and rows <= 2 * slots:
        return direct(forcing, inflow, self_solve, greens, kept_cols, counts)
    return gathering(forcing, inflow, self_solve, greens, kept_cols, counts)


def solution(mesh):
    placed = (
        P("slab", "row", None),
        P("row", None),
        P("slab", "row", None, None),
        P("slab", "row", None, None, None),
        P("slab", "row", None),
        P("slab", "row"),
    )
    return jax.shard_map(
        shards, mesh=mesh, in_specs=placed, out_specs=P("slab", "row", None), check_vma=False
    )
```

```python
import functools

import jax
import jax.numpy as jnp
from jax import lax
from jax.experimental import pallas as pl
from jax.experimental.pallas import tpu as pltpu
from jax.sharding import PartitionSpec as P

CORES = 2
VMEM_LIMIT = 48 * 2**20
LAST_LAST = (((1,), (1,)), ((), ()))
LAST_FIRST = (((1,), (0,)), ((), ()))
FIRST_LAST = (((0,), (1,)), ((), ()))
IN_VMEM = pl.BlockSpec(memory_space=pltpu.VMEM)
IN_SMEM = pl.BlockSpec(memory_space=pltpu.SMEM)
ANYWHERE = pl.BlockSpec(memory_space=pl.ANY)


def params():
    return pltpu.CompilerParams(vmem_limit_bytes=VMEM_LIMIT)


def step_of(order, chips):
    half = chips // 2
    return half + order // 2 if order % 2 == 0 else half - 1 - order // 2


def order_of(step, chips):
    half = chips // 2
    return jnp.where(step >= half, 2 * (step - half), 2 * (half - 1 - step) + 1)


def position_of(slot, chips, cols_ref):
    me = lax.axis_index("row")
    chip, core = me // CORES, me % CORES
    column = cols_ref[0, 0, slot]
    return jnp.where(column % CORES == core, 0, chips) + order_of(chip ^ (column // CORES), chips)


def place_kernel(chips, cols_in, count_ref, greens_ref, solve_in, source_in, *refs):
    slots_ref, held_ref, solve_ref, source_ref, cols_ref, sems = refs
    slots, positions = greens_ref.shape[2], slots_ref.shape[0]
    table = pltpu.make_async_copy(cols_in, cols_ref, sems.at[0])
    copies = [
        pltpu.make_async_copy(greens_ref.at[0, 0], held_ref, sems.at[1]),
        pltpu.make_async_copy(solve_in.at[0, 0], solve_ref, sems.at[2]),
        pltpu.make_async_copy(source_in, source_ref, sems.at[3]),
    ]
    first = lax.axis_index("slab") == 0
    table.start()

    @pl.when(first)
    def _():
        for copy in copies:
            copy.start()

    for position in range(positions):
        slots_ref[position] = -1
    table.wait()
    for slot in range(slots):

        @pl.when(slot < count_ref[0, 0])
        def _():
            slots_ref[position_of(slot, chips, cols_ref)] = slot

    @pl.when(first)
    def _():
        for copy in copies:
            copy.wait()


def place(chips, cols, count, greens, solve, source):
    slots, rows, depth = greens.shape[2:]
    return pl.pallas_call(
        functools.partial(place_kernel, chips),
        out_shape=(
            pltpu.SMEM((chips * CORES,), jnp.int32),
            pltpu.VMEM((slots, rows, depth), greens.dtype),
            pltpu.VMEM(solve.shape[2:], solve.dtype),
            pltpu.VMEM(source.shape, source.dtype),
        ),
        in_specs=[ANYWHERE, IN_SMEM] + [ANYWHERE] * 3,
        out_specs=(IN_SMEM,) + (IN_VMEM,) * 3,
        scratch_shapes=[
            pltpu.SMEM(cols.shape, cols.dtype),
            pltpu.SemaphoreType.DMA((4,)),
        ],
        compiler_params=params(),
        cost_estimate=pl.CostEstimate(flops=0, bytes_accessed=2 * greens.size * 2, transcendentals=0),
        name="place",
    )(cols, count, greens, solve, source)


def fold_kernel(section, slots_ref, greens_ref, solve_in, source_in, folded_ref, base_ref, held_ref, solve_ref, source_ref, sems):
    @pl.when(lax.axis_index("slab") == section)
    def _():
        copies = [
            pltpu.make_async_copy(greens_ref.at[0, 0], held_ref, sems.at[0]),
            pltpu.make_async_copy(solve_in.at[0, 0], solve_ref, sems.at[1]),
            pltpu.make_async_copy(source_in, source_ref, sems.at[2]),
        ]
        for copy in copies:
            copy.start()
        for copy in copies:
            copy.wait()
        base_ref[...] = lax.dot_general(source_ref[...], solve_ref[...], LAST_LAST, preferred_element_type=jnp.float32)

        for position in range(folded_ref.shape[0]):
            slot = slots_ref[position]
            solved = lax.dot_general(
                held_ref[jnp.maximum(slot, 0)], solve_ref[...], FIRST_LAST, preferred_element_type=jnp.float32
            )
            folded_ref[position] = jnp.where(slot >= 0, solved, jnp.zeros_like(solved)).astype(folded_ref.dtype)


def fold(section, slots, greens, solve, source):
    held, rows, depth = greens.shape[2:]
    return pl.pallas_call(
        functools.partial(fold_kernel, section),
        out_shape=(
            pltpu.VMEM((*slots.shape, depth, rows), greens.dtype),
            pltpu.VMEM(source.shape, jnp.float32),
        ),
        in_specs=[IN_SMEM] + [ANYWHERE] * 3,
        out_specs=(IN_VMEM,) * 2,
        scratch_shapes=[
            pltpu.VMEM((held, rows, depth), greens.dtype),
            pltpu.VMEM(solve.shape[2:], solve.dtype),
            pltpu.VMEM(source.shape, source.dtype),
            pltpu.SemaphoreType.DMA((3,)),
        ],
        compiler_params=params(),
        cost_estimate=pl.CostEstimate(
            flops=2 * greens.size * rows, bytes_accessed=2 * greens.size * 2, transcendentals=0
        ),
        name="fold",
    )(slots, greens, solve, source)


def products(tiles, positions, placed_ref, slots_ref, total):
    for tile, position in zip(tiles, positions):
        if slots_ref is None:
            total += jnp.dot(tile[...], placed_ref[position], preferred_element_type=jnp.float32)
        else:
            slot = slots_ref[position]
            used = jnp.where(slot >= 0, tile[...], jnp.zeros_like(tile))
            total += lax.dot_general(
                used, placed_ref[jnp.maximum(slot, 0)], LAST_LAST, preferred_element_type=jnp.float32
            )
    return total


def early_kernel(section, positions, *refs):
    slots_ref, refs = (refs[0], refs[1:]) if section == 0 else (None, refs)
    placed_ref, before_ref, tiles, total_ref = refs[0], refs[1], refs[2:-1], refs[-1]

    @pl.when(lax.axis_index("slab") == section)
    def _():
        before = before_ref[...].astype(jnp.float32)
        total_ref[...] = products(tiles, positions, placed_ref, slots_ref, before)


def early(section, positions, slots, placed, before, tiles):
    scalars = [slots] if section == 0 else []
    return pl.pallas_call(
        functools.partial(early_kernel, section, positions),
        out_shape=pltpu.VMEM(before.shape, jnp.float32),
        in_specs=[IN_SMEM] * len(scalars) + [IN_VMEM] * (2 + len(tiles)),
        out_specs=IN_VMEM,
        compiler_params=params(),
        name="early_tiles",
    )(*scalars, placed, before, *tiles)


def late_kernel(section, position, *refs):
    slots_ref, refs = (refs[0], refs[1:]) if section == 0 else (None, refs)
    placed_ref, total_ref, tile_ref, solve_ref, trace_ref = *refs[:3], refs[3], refs[-1]

    @pl.when(lax.axis_index("slab") == section)
    def _():
        total = products([tile_ref], [position], placed_ref, slots_ref, total_ref[...])
        if section == 0:
            coupled = total.astype(jnp.bfloat16)
            total = lax.dot_general(coupled, solve_ref[...], LAST_LAST, preferred_element_type=jnp.float32)
        trace_ref[...] = total.astype(trace_ref.dtype)


def late(section, position, slots, placed, total, tile, solve, trace):
    scalars = [slots] if section == 0 else []
    operands = [placed, total, tile, *([solve] if section == 0 else []), trace]
    return pl.pallas_call(
        functools.partial(late_kernel, section, position),
        out_shape=pltpu.VMEM(trace.shape, trace.dtype),
        in_specs=[IN_SMEM] * len(scalars) + [IN_VMEM] * len(operands),
        out_specs=IN_VMEM,
        input_output_aliases={len(scalars) + len(operands) - 1: 0},
        compiler_params=params(),
        name="late_tile",
    )(*scalars, *operands)


def swapped(tile, rows):
    return lax.ppermute(tile, "row", [(r, r ^ 1) for r in range(rows)])


def sent(tile, source, target, step, slabs, rows, via):
    partner = [r ^ (step * CORES) for r in range(rows)]
    pairs = [(source * rows + r, target * rows + partner[r]) for r in range(rows)]
    if via is not None:
        path = [target, *via, source] if source != target else [source]
        for here, there in zip(path, path[1:]):
            pairs += [(here * rows + r, there * rows + (r if via else partner[r])) for r in range(rows)]
        pairs += [(s * rows + r, s * rows + (r ^ 1)) for s in range(slabs) if s not in path for r in range(rows)]
    return lax.ppermute(tile, ("slab", "row"), pairs)


def ways(section, slabs, chips):
    others = [s % slabs for s in range(section + 1, section + slabs - 1)]
    if len(others) < 2 or chips < 4:
        return [None] * chips
    free, late = others[0], others[-1]
    if section < slabs - 1:
        return [(free,)] + [None] * (chips - 1)
    return [(free,), (late, free)] + [None] * (chips - 3) + [()]


def direct(forcing, inflow, self_solve, greens, kept_cols, counts):
    slabs, rows = lax.axis_size("slab"), lax.axis_size("row")
    chips, last = rows // CORES, slabs - 1
    steps = [step_of(order, chips) for order in range(chips)]
    entering, source = inflow.T, forcing[0].T
    kept_cols, greens, self_solve, source = (
        pltpu.with_memory_space_constraint(array, pltpu.HBM) for array in (kept_cols, greens, self_solve, source)
    )
    slots, placed, solve, base = place(chips, kept_cols, counts, greens, self_solve, source)
    given = (slots, greens, self_solve, source)
    ready = fold(last, *given) if last > 0 else ()
    trace = jnp.zeros(entering.shape, jnp.bfloat16)
    for section in range(slabs):
        if section == 0:
            own = [sent(entering, 0, 0, step, slabs, rows, ()) for step in steps if step]
            placed, base, solve, *ready, own[0] = lax.optimization_barrier((placed, base, solve, *ready, own[0]))
            orders = [steps.index(0)] + [order for order, step in enumerate(steps) if step]
            own = [entering] + own
        else:
            vias = ways(section, slabs, chips)
            own = [sent(trace, section - 1, section, step, slabs, rows, via) for step, via in zip(steps, vias)]
            orders = list(range(chips))
            if section < last:
                placed, base = fold(section, *given)
                placed, base, own[0] = lax.optimization_barrier((placed, base, own[0]))
            else:
                placed, base = ready
        if section == 0:
            other = [swapped(tile, rows) for tile in own[:-1]]
            held = [(own[0], orders[0]), (other[0], chips + orders[0])]
            tiles, positions = zip(*held)
            total = early(section, positions, slots, placed, base, tiles)
            own[1], total = lax.optimization_barrier((own[1], total))
            other.append(swapped(own[-1], rows))
            held = [(own[i], orders[i]) for i in range(1, chips)] + [(other[i], chips + orders[i]) for i in range(1, chips - 1)]
            tiles, positions = zip(*held)
            total = early(section, positions, slots, placed, total, tiles)
            arriving = [(None, chips + orders[-1])]
        else:
            other = [swapped(tile, rows) for tile in own]
            arriving = []
            for order, *both in zip(orders, own, other):
                arriving += [(tile, side * chips + order) for side, tile in enumerate(both)]
            total = base
            for first in [0, *range(3, len(arriving) - 1, 2)]:
                tiles, positions = zip(*arriving[first : first + 3 if first == 0 else first + 2])
                total = early(section, positions, slots, placed, total, tiles)
        trace = late(section, arriving[-1][1], slots, placed, total, other[-1], solve, trace)
    return trace.T[None]


def shifted(array, axis, by):
    size = lax.axis_size(axis)
    return lax.ppermute(array, axis, [(i, i + by) for i in range(size) if 0 <= i + by < size])


def gathering(forcing, inflow, self_solve, greens, kept_cols, counts):
    source, green_row, solve = forcing[0], greens[0, 0], self_solve[0, 0]
    valid = jnp.arange(green_row.shape[0], dtype=jnp.int32) < counts[0, 0]
    incoming = inflow
    for section in range(lax.axis_size("slab")):
        if section > 0:
            arrived = shifted(trace, "slab", 1)
            incoming = jnp.where(lax.axis_index("slab") == 0, inflow, arrived)
        gathered = lax.all_gather(incoming, "row", axis=0)
        chosen = gathered[kept_cols[0, 0]]
        chosen = jnp.where(valid[:, None, None], chosen, jnp.zeros((), chosen.dtype))
        total = jnp.einsum("kij,kjw->iw", green_row, chosen, preferred_element_type=jnp.float32)
        coupled = (total + source.astype(jnp.float32)).astype(jnp.bfloat16)
        trace = jnp.dot(solve, coupled, preferred_element_type=jnp.float32).astype(jnp.bfloat16)
    return trace[None]


def shards(forcing, inflow, self_solve, greens, kept_cols, counts):
    rows, slots = lax.axis_size("row"), greens.shape[2]
    chips = rows // CORES
    if rows == chips * CORES and chips & (chips - 1) == 0 and 1 < chips and rows <= 2 * slots:
        return direct(forcing, inflow, self_solve, greens, kept_cols, counts)
    return gathering(forcing, inflow, self_solve, greens, kept_cols, counts)


def solution(mesh):
    placed = (
        P("slab", "row", None),
        P("row", None),
        P("slab", "row", None, None),
        P("slab", "row", None, None, None),
        P("slab", "row", None),
        P("slab", "row"),
    )
    return jax.shard_map(
        shards, mesh=mesh, in_specs=placed, out_specs=P("slab", "row", None), check_vma=False
    )
```

```python
import functools

import jax
import jax.numpy as jnp
from jax import lax
from jax.experimental import pallas as pl
from jax.experimental.pallas import tpu as pltpu
from jax.sharding import PartitionSpec as P

CORES = 2
VMEM_LIMIT = 48 * 2**20
LAST_LAST = (((1,), (1,)), ((), ()))
LAST_FIRST = (((1,), (0,)), ((), ()))
FIRST_LAST = (((0,), (1,)), ((), ()))
IN_VMEM = pl.BlockSpec(memory_space=pltpu.VMEM)
IN_SMEM = pl.BlockSpec(memory_space=pltpu.SMEM)
ANYWHERE = pl.BlockSpec(memory_space=pl.ANY)


def params():
    return pltpu.CompilerParams(vmem_limit_bytes=VMEM_LIMIT)


def step_of(order, chips):
    half = chips // 2
    return half + order // 2 if order % 2 == 0 else half - 1 - order // 2


def order_of(step, chips):
    half = chips // 2
    return jnp.where(step >= half, 2 * (step - half), 2 * (half - 1 - step) + 1)


def position_of(slot, chips, cols_ref):
    me = lax.axis_index("row")
    chip, core = me // CORES, me % CORES
    column = cols_ref[0, 0, slot]
    return jnp.where(column % CORES == core, 0, chips) + order_of(chip ^ (column // CORES), chips)


def place_kernel(chips, cols_in, count_ref, greens_ref, solve_in, source_in, *refs):
    slots_ref, held_ref, solve_ref, source_ref, cols_ref, sems = refs
    slots, positions = greens_ref.shape[2], slots_ref.shape[0]
    table = pltpu.make_async_copy(cols_in, cols_ref, sems.at[0])
    copies = [
        pltpu.make_async_copy(greens_ref.at[0, 0], held_ref, sems.at[1]),
        pltpu.make_async_copy(solve_in.at[0, 0], solve_ref, sems.at[2]),
        pltpu.make_async_copy(source_in, source_ref, sems.at[3]),
    ]
    first = lax.axis_index("slab") == 0
    table.start()

    @pl.when(first)
    def _():
        for copy in copies:
            copy.start()

    for position in range(positions):
        slots_ref[position] = -1
    table.wait()
    for slot in range(slots):

        @pl.when(slot < count_ref[0, 0])
        def _():
            slots_ref[position_of(slot, chips, cols_ref)] = slot

    @pl.when(first)
    def _():
        for copy in copies:
            copy.wait()


def place(chips, cols, count, greens, solve, source):
    slots, rows, depth = greens.shape[2:]
    return pl.pallas_call(
        functools.partial(place_kernel, chips),
        out_shape=(
            pltpu.SMEM((chips * CORES,), jnp.int32),
            pltpu.VMEM((slots, rows, depth), greens.dtype),
            pltpu.VMEM(solve.shape[2:], solve.dtype),
            pltpu.VMEM(source.shape, source.dtype),
        ),
        in_specs=[ANYWHERE, IN_SMEM] + [ANYWHERE] * 3,
        out_specs=(IN_SMEM,) + (IN_VMEM,) * 3,
        scratch_shapes=[
            pltpu.SMEM(cols.shape, cols.dtype),
            pltpu.SemaphoreType.DMA((4,)),
        ],
        compiler_params=params(),
        cost_estimate=pl.CostEstimate(flops=0, bytes_accessed=2 * greens.size * 2, transcendentals=0),
        name="place",
    )(cols, count, greens, solve, source)


def fold_kernel(section, slots_ref, greens_ref, solve_in, source_in, folded_ref, base_ref, held_ref, solve_ref, source_ref, sems):
    @pl.when(lax.axis_index("slab") == section)
    def _():
        copies = [
            pltpu.make_async_copy(greens_ref.at[0, 0], held_ref, sems.at[0]),
            pltpu.make_async_copy(solve_in.at[0, 0], solve_ref, sems.at[1]),
            pltpu.make_async_copy(source_in, source_ref, sems.at[2]),
        ]
        for copy in copies:
            copy.start()
        for copy in copies:
            copy.wait()
        base_ref[...] = lax.dot_general(source_ref[...], solve_ref[...], LAST_LAST, preferred_element_type=jnp.float32)

        def fold_one(position, carry):
            slot = slots_ref[position]
            solved = lax.dot_general(
                held_ref[jnp.maximum(slot, 0)], solve_ref[...], FIRST_LAST, preferred_element_type=jnp.float32
            )
            folded_ref[position] = jnp.where(slot >= 0, solved, jnp.zeros_like(solved)).astype(folded_ref.dtype)
            return carry

        lax.fori_loop(0, folded_ref.shape[0], fold_one, 0, unroll=section != lax.axis_size("slab") - 1)


def fold(section, slots, greens, solve, source):
    held, rows, depth = greens.shape[2:]
    return pl.pallas_call(
        functools.partial(fold_kernel, section),
        out_shape=(
            pltpu.VMEM((*slots.shape, depth, rows), greens.dtype),
            pltpu.VMEM(source.shape, jnp.float32),
        ),
        in_specs=[IN_SMEM] + [ANYWHERE] * 3,
        out_specs=(IN_VMEM,) * 2,
        scratch_shapes=[
            pltpu.VMEM((held, rows, depth), greens.dtype),
            pltpu.VMEM(solve.shape[2:], solve.dtype),
            pltpu.VMEM(source.shape, source.dtype),
            pltpu.SemaphoreType.DMA((3,)),
        ],
        compiler_params=params(),
        cost_estimate=pl.CostEstimate(
            flops=2 * greens.size * rows, bytes_accessed=2 * greens.size * 2, transcendentals=0
        ),
        name="fold",
    )(slots, greens, solve, source)


def products(tiles, positions, placed_ref, slots_ref, total):
    for tile, position in zip(tiles, positions):
        if slots_ref is None:
            total += jnp.dot(tile[...], placed_ref[position], preferred_element_type=jnp.float32)
        else:
            slot = slots_ref[position]
            used = jnp.where(slot >= 0, tile[...], jnp.zeros_like(tile))
            total += lax.dot_general(
                used, placed_ref[jnp.maximum(slot, 0)], LAST_LAST, preferred_element_type=jnp.float32
            )
    return total


def early_kernel(section, positions, *refs):
    slots_ref, refs = (refs[0], refs[1:]) if section == 0 else (None, refs)
    placed_ref, before_ref, tiles, total_ref = refs[0], refs[1], refs[2:-1], refs[-1]

    @pl.when(lax.axis_index("slab") == section)
    def _():
        before = before_ref[...].astype(jnp.float32)
        total_ref[...] = products(tiles, positions, placed_ref, slots_ref, before)


def early(section, positions, slots, placed, before, tiles):
    scalars = [slots] if section == 0 else []
    return pl.pallas_call(
        functools.partial(early_kernel, section, positions),
        out_shape=pltpu.VMEM(before.shape, jnp.float32),
        in_specs=[IN_SMEM] * len(scalars) + [IN_VMEM] * (2 + len(tiles)),
        out_specs=IN_VMEM,
        compiler_params=params(),
        name="early_tiles",
    )(*scalars, placed, before, *tiles)


def late_kernel(section, position, *refs):
    slots_ref, refs = (refs[0], refs[1:]) if section == 0 else (None, refs)
    placed_ref, total_ref, tile_ref, solve_ref, trace_ref = *refs[:3], refs[3], refs[-1]

    @pl.when(lax.axis_index("slab") == section)
    def _():
        total = products([tile_ref], [position], placed_ref, slots_ref, total_ref[...])
        if section == 0:
            coupled = total.astype(jnp.bfloat16)
            total = lax.dot_general(coupled, solve_ref[...], LAST_LAST, preferred_element_type=jnp.float32)
        trace_ref[...] = total.astype(trace_ref.dtype)


def late(section, position, slots, placed, total, tile, solve, trace):
    scalars = [slots] if section == 0 else []
    operands = [placed, total, tile, *([solve] if section == 0 else []), trace]
    return pl.pallas_call(
        functools.partial(late_kernel, section, position),
        out_shape=pltpu.VMEM(trace.shape, trace.dtype),
        in_specs=[IN_SMEM] * len(scalars) + [IN_VMEM] * len(operands),
        out_specs=IN_VMEM,
        input_output_aliases={len(scalars) + len(operands) - 1: 0},
        compiler_params=params(),
        name="late_tile",
    )(*scalars, *operands)


def swapped(tile, rows):
    return lax.ppermute(tile, "row", [(r, r ^ 1) for r in range(rows)])


def sent(tile, source, target, step, slabs, rows, via):
    partner = [r ^ (step * CORES) for r in range(rows)]
    pairs = [(source * rows + r, target * rows + partner[r]) for r in range(rows)]
    if via is not None:
        path = [target, *via, source] if source != target else [source]
        for here, there in zip(path, path[1:]):
            pairs += [(here * rows + r, there * rows + (r if via else partner[r])) for r in range(rows)]
        pairs += [(s * rows + r, s * rows + (r ^ 1)) for s in range(slabs) if s not in path for r in range(rows)]
    return lax.ppermute(tile, ("slab", "row"), pairs)


def ways(section, slabs, chips):
    others = [s % slabs for s in range(section + 1, section + slabs - 1)]
    if len(others) < 2 or chips < 4:
        return [None] * chips
    free, late = others[0], others[-1]
    if section < slabs - 1:
        return [(free,)] + [None] * (chips - 1)
    return [(free,), (late, free)] + [None] * (chips - 3) + [()]


def direct(forcing, inflow, self_solve, greens, kept_cols, counts):
    slabs, rows = lax.axis_size("slab"), lax.axis_size("row")
    chips, last = rows // CORES, slabs - 1
    steps = [step_of(order, chips) for order in range(chips)]
    entering, source = inflow.T, forcing[0].T
    kept_cols, greens, self_solve, source = (
        pltpu.with_memory_space_constraint(array, pltpu.HBM) for array in (kept_cols, greens, self_solve, source)
    )
    slots, placed, solve, base = place(chips, kept_cols, counts, greens, self_solve, source)
    given = (slots, greens, self_solve, source)
    ready = fold(last, *given) if last > 0 else ()
    trace = jnp.zeros(entering.shape, jnp.bfloat16)
    for section in range(slabs):
        if section == 0:
            own = [sent(entering, 0, 0, step, slabs, rows, ()) for step in steps if step]
            placed, base, solve, *ready, own[0] = lax.optimization_barrier((placed, base, solve, *ready, own[0]))
            orders = [steps.index(0)] + [order for order, step in enumerate(steps) if step]
            own = [entering] + own
        else:
            vias = ways(section, slabs, chips)
            own = [sent(trace, section - 1, section, step, slabs, rows, via) for step, via in zip(steps, vias)]
            orders = list(range(chips))
            if section < last:
                placed, base = fold(section, *given)
                placed, base, own[0] = lax.optimization_barrier((placed, base, own[0]))
            else:
                placed, base = ready
        if section == 0:
            other = [swapped(tile, rows) for tile in own[:-1]]
            held = [(own[0], orders[0]), (other[0], chips + orders[0])]
            tiles, positions = zip(*held)
            total = early(section, positions, slots, placed, base, tiles)
            own[1], total = lax.optimization_barrier((own[1], total))
            other.append(swapped(own[-1], rows))
            held = [(own[i], orders[i]) for i in range(1, chips)] + [(other[i], chips + orders[i]) for i in range(1, chips - 1)]
            tiles, positions = zip(*held)
            total = early(section, positions, slots, placed, total, tiles)
            arriving = [(None, chips + orders[-1])]
        else:
            other = [swapped(tile, rows) for tile in own]
            arriving = []
            for order, *both in zip(orders, own, other):
                arriving += [(tile, side * chips + order) for side, tile in enumerate(both)]
            total = base
            for first in [0, *range(3, len(arriving) - 1, 2)]:
                tiles, positions = zip(*arriving[first : first + 3 if first == 0 else first + 2])
                total = early(section, positions, slots, placed, total, tiles)
        trace = late(section, arriving[-1][1], slots, placed, total, other[-1], solve, trace)
    return trace.T[None]


def shifted(array, axis, by):
    size = lax.axis_size(axis)
    return lax.ppermute(array, axis, [(i, i + by) for i in range(size) if 0 <= i + by < size])


def gathering(forcing, inflow, self_solve, greens, kept_cols, counts):
    source, green_row, solve = forcing[0], greens[0, 0], self_solve[0, 0]
    valid = jnp.arange(green_row.shape[0], dtype=jnp.int32) < counts[0, 0]
    incoming = inflow
    for section in range(lax.axis_size("slab")):
        if section > 0:
            arrived = shifted(trace, "slab", 1)
            incoming = jnp.where(lax.axis_index("slab") == 0, inflow, arrived)
        gathered = lax.all_gather(incoming, "row", axis=0)
        chosen = gathered[kept_cols[0, 0]]
        chosen = jnp.where(valid[:, None, None], chosen, jnp.zeros((), chosen.dtype))
        total = jnp.einsum("kij,kjw->iw", green_row, chosen, preferred_element_type=jnp.float32)
        coupled = (total + source.astype(jnp.float32)).astype(jnp.bfloat16)
        trace = jnp.dot(solve, coupled, preferred_element_type=jnp.float32).astype(jnp.bfloat16)
    return trace[None]


def shards(forcing, inflow, self_solve, greens, kept_cols, counts):
    rows, slots = lax.axis_size("row"), greens.shape[2]
    chips = rows // CORES
    if rows == chips * CORES and chips & (chips - 1) == 0 and 1 < chips and rows <= 2 * slots:
        return direct(forcing, inflow, self_solve, greens, kept_cols, counts)
    return gathering(forcing, inflow, self_solve, greens, kept_cols, counts)


def solution(mesh):
    placed = (
        P("slab", "row", None),
        P("row", None),
        P("slab", "row", None, None),
        P("slab", "row", None, None, None),
        P("slab", "row", None),
        P("slab", "row"),
    )
    return jax.shard_map(
        shards, mesh=mesh, in_specs=placed, out_specs=P("slab", "row", None), check_vma=False
    )
```
